32 devices in a mesh: grp: 2 (over y), ax: 8 (over z, x), ch: 2 (over core).
Axes of the slice: x: 2, y: 2, z: 4, core: 2. Of those that a mesh axis runs over, the one named last changes fastest.
Arguments:
- pair_first: bfloat16 [32, 16, 128], P(('grp', 'ax')), parts along dimension 0, may hold values from -6 to 6
- pair_second: bfloat16 [32, 16, 128], P(('grp', 'ax')), parts along dimension 0, may hold values from -6 to 6
- grad_out: bfloat16 [32, 16, 128], P(('grp', 'ax')), parts along dimension 0, may hold values from -6 to 6
- norm_gain: float32 [2, 128], replicated, may hold values from 0.1 to 1.9
- proj_weight: bfloat16 [2, 128, 512], replicated, may hold values from -0.5 to 0.5
- gate_weight: bfloat16 [2, 128, 128], replicated, may hold values from -0.5 to 0.5
- out_gain: float32 [2, 128], replicated, may hold values from 0.1 to 1.9
- out_weight: bfloat16 [2, 128, 128], replicated, may hold values from -0.5 to 0.5
Outputs:
- grad_in: bfloat16 [32, 16, 128], P(('grp', 'ax')), parts along dimension 0
- grad_proj: float32 [4, 128, 512], P('grp'), parts along dimension 0
- grad_gate: float32 [4, 128, 128], P('grp'), parts along dimension 0
- grad_out_weight: float32 [4, 128, 128], P('grp'), parts along dimension 0
The draws below stay inside these ranges and needn't reach their ends.
There are 2 independent parts, one for each index of `grp`. The reference program is written for one: setup_inputs(seed, part) draws one part's arguments, and reference() takes and returns one part's arrays. A program takes and returns all parts, laid end to end along the dimension named above; an argument that names none is the same for every part. Nothing has to cross between parts.
All inputs are finite; a program needn't handle non-finite values.
Results may differ from the reference program's by a relative error of at most 0.017.
Values may be sent and summed in bfloat16 or wider, within the bound.
A program may use at most 128 MiB of HBM per device.

```python
import jax
import jax.numpy as jnp
from jax import lax

C = 128
CH = 128
N = 16


def block_scale(stream_key, shape, pieces, least, largest):
    def one(position, shards_of):
        draws = jax.random.uniform(jax.random.fold_in(jax.random.fold_in(stream_key, 6), position), (shards_of,), jnp.float32, least / len(pieces), largest / len(pieces))
        return jnp.repeat(jnp.exp(draws), shape[position] // shards_of).reshape((-1,) + (1,) * (len(shape) - position - 1))

    loudness = one(*pieces[0])
    for cut in pieces[1:]:
        loudness = loudness * one(*cut)
    return loudness


def centred(rng, extent, scale, limit, cuts=(), held_as=jnp.bfloat16):
    result = scale * jax.random.normal(rng, extent, jnp.float32)
    if cuts:
        result = result * block_scale(rng, extent, cuts, -0.22, 0.18)
    return jnp.clip(result, -limit, limit).astype(held_as)


def setup_inputs(seed: int = 0, part: int = 0) -> dict:
    arg_keys = jax.random.split(jax.random.key(seed), 9)
    part_splits = jax.random.split(jax.random.fold_in(arg_keys[8], part), 9)
    pair_first = centred(part_splits[0], (N, N, C), 1.0, 6.0, ((0, 8),))
    pair_second = centred(part_splits[1], (N, N, C), 1.0, 6.0, ((0, 8),))
    grad_out = centred(part_splits[2], (N, N, C), 1.0, 6.0, ((0, 8),))
    norm_gain = jnp.clip(1.0 + 0.18 * jax.random.normal(arg_keys[3], (2, C), jnp.float32), 0.1, 1.9)
    proj_weight = centred(arg_keys[4], (2, C, 4 * CH), C ** -0.5, 0.5)
    gate_weight = centred(arg_keys[5], (2, C, C), C ** -0.5, 0.5)
    out_gain = jnp.clip(1.0 + 0.18 * jax.random.normal(arg_keys[6], (2, CH), jnp.float32), 0.1, 1.9)
    out_weight = centred(arg_keys[7], (2, CH, C), CH ** -0.5, 0.5)
    return dict(pair_first=pair_first, pair_second=pair_second, grad_out=grad_out, norm_gain=norm_gain, proj_weight=proj_weight, gate_weight=gate_weight, out_gain=out_gain, out_weight=out_weight)


EPS = 1e-05

def normalize(values, axis):
    center = values - lax.optimization_barrier(jnp.mean(values, axis=axis, keepdims=True))
    scale = lax.rsqrt(lax.optimization_barrier(jnp.mean(center * center, axis=axis, keepdims=True)) + EPS)
    return (center * scale, scale)

def norm_back(grad, normed, scale, axis):
    return scale * (grad - lax.optimization_barrier(jnp.mean(grad, axis=axis, keepdims=True)) - normed * lax.optimization_barrier(jnp.mean(grad * normed, axis=axis, keepdims=True)))

def widen(form, first, second):
    return jnp.einsum(form, first.astype(jnp.float32), second.astype(jnp.float32), precision=lax.Precision.HIGHEST)

def layer_grad(pair, cotangent, layer_gain, w_proj, w_gate, layer_out_gain, w_out, incoming):
    width = w_out.shape[0]
    count = pair.shape[0]
    pair_hat, pair_scale = normalize(pair.astype(jnp.float32), 2)
    flat_normed = (pair_hat * layer_gain).astype(jnp.bfloat16).reshape(-1, pair.shape[2])
    projected = jnp.dot(flat_normed, w_proj, preferred_element_type=jnp.float32)
    gate_sig = jax.nn.sigmoid(jnp.dot(flat_normed, w_gate, preferred_element_type=jnp.float32))
    sig_a = jax.nn.sigmoid(projected[:, width:2 * width])
    sig_b = jax.nn.sigmoid(projected[:, 3 * width:])
    left_side = (sig_a * projected[:, :width]).astype(jnp.bfloat16).reshape(count, count, width).transpose(2, 0, 1)
    right_side = (sig_b * projected[:, 2 * width:3 * width]).astype(jnp.bfloat16).reshape(count, count, width).transpose(2, 0, 1)
    if incoming:
        tri = widen('cki,ckj->cij', left_side, right_side)
    else:
        tri = widen('cik,cjk->cij', left_side, right_side)
    tri_hat, tri_scale = normalize(tri, 0)
    tri_norm = (tri_hat * layer_out_gain[:, None, None]).astype(jnp.bfloat16)
    linear = widen('cij,cd->ijd', tri_norm, w_out).reshape(-1, w_out.shape[1])
    flat_cot = cotangent.reshape(-1, cotangent.shape[2])
    d_linear = (flat_cot * gate_sig).astype(jnp.bfloat16)
    d_gate = (flat_cot * linear * gate_sig * (1.0 - gate_sig)).astype(jnp.bfloat16)
    d_cube = d_linear.reshape(count, count, -1)
    d_norm = widen('ijd,cd->cij', d_cube, w_out)
    g_out = widen('cij,ijd->cd', tri_norm, d_cube)
    tri_grad = norm_back(d_norm * layer_out_gain[:, None, None], tri_hat, tri_scale, 0).astype(jnp.bfloat16)
    if incoming:
        d_left = widen('ckj,cij->cki', right_side, tri_grad)
        d_right = widen('cki,cij->ckj', left_side, tri_grad)
    else:
        d_left = widen('cij,cjk->cik', tri_grad, right_side)
        d_right = widen('cij,cik->cjk', tri_grad, left_side)
    flat_left = d_left.transpose(1, 2, 0).reshape(-1, width)
    flat_right = d_right.transpose(1, 2, 0).reshape(-1, width)
    d_proj = jnp.concatenate([flat_left * sig_a, flat_left * projected[:, :width] * sig_a * (1.0 - sig_a), flat_right * sig_b, flat_right * projected[:, 2 * width:3 * width] * sig_b * (1.0 - sig_b)], axis=1).astype(jnp.bfloat16)
    d_normed = jnp.dot(d_proj, w_proj.T, preferred_element_type=jnp.float32) + jnp.dot(d_gate, w_gate.T, preferred_element_type=jnp.float32)
    g_proj = jnp.dot(flat_normed.T, d_proj, preferred_element_type=jnp.float32)
    g_gate = jnp.dot(flat_normed.T, d_gate, preferred_element_type=jnp.float32)
    d_pair = cotangent + norm_back(d_normed.reshape(cotangent.shape) * layer_gain, pair_hat, pair_scale, 2)
    return (d_pair, g_proj, g_gate, g_out)

def reference(pair_first, pair_second, grad_out, norm_gain, proj_weight, gate_weight, out_gain, out_weight):
    second = layer_grad(pair_second, grad_out.astype(jnp.float32), norm_gain[1], proj_weight[1], gate_weight[1], out_gain[1], out_weight[1], True)
    carried = lax.optimization_barrier(second[0].astype(jnp.bfloat16)).astype(jnp.float32)
    first = layer_grad(pair_first, carried, norm_gain[0], proj_weight[0], gate_weight[0], out_gain[0], out_weight[0], False)
    count = pair_first.shape[1]
    grad_in = first[0].astype(jnp.bfloat16)
    grad_proj = jnp.stack([first[1], second[1]]) / count
    grad_gate = jnp.stack([first[2], second[2]]) / count
    grad_out_weight = jnp.stack([first[3], second[3]]) / count
    return (grad_in, grad_proj, grad_gate, grad_out_weight)
```

```python
import functools

import jax
import jax.numpy as jnp
from jax import lax
from jax.experimental import pallas as pl
from jax.experimental.pallas import tpu as pltpu
from jax.sharding import PartitionSpec as P

EPS = 1e-05


def normalize(values, axis):
    center = values - jnp.mean(values, axis=axis, keepdims=True)
    scale = lax.rsqrt(jnp.mean(center * center, axis=axis, keepdims=True) + EPS)
    return (center * scale, scale)


def norm_back(grad, normed, scale, axis):
    return scale * (
        grad
        - jnp.mean(grad, axis=axis, keepdims=True)
        - normed * jnp.mean(grad * normed, axis=axis, keepdims=True)
    )


def own_cells(values):
    share = values.shape[1] // lax.axis_size("ch")
    return lax.dynamic_slice_in_dim(values, lax.axis_index("ch") * share, share, 1)


def front(pair, layer_gain, w_proj, w_gate):
    width = w_proj.shape[1] // 4
    rows = pair.shape[0]
    count = pair.shape[1]
    pair_hat, pair_scale = normalize(pair.astype(jnp.float32), 2)
    flat_normed = (pair_hat * layer_gain).astype(jnp.bfloat16).reshape(-1, pair.shape[2])
    projected = jnp.dot(flat_normed, w_proj, preferred_element_type=jnp.float32)
    gate_sig = jax.nn.sigmoid(jnp.dot(flat_normed, w_gate, preferred_element_type=jnp.float32))
    sig_a = jax.nn.sigmoid(projected[:, width : 2 * width])
    sig_b = jax.nn.sigmoid(projected[:, 3 * width :])
    left_side = (
        (sig_a * projected[:, :width])
        .astype(jnp.bfloat16)
        .reshape(rows, count, width)
        .transpose(2, 0, 1)
    )
    right_side = (
        (sig_b * projected[:, 2 * width : 3 * width])
        .astype(jnp.bfloat16)
        .reshape(rows, count, width)
        .transpose(2, 0, 1)
    )
    left_half, right_half = (
        lax.all_to_all(left_side, "ch", split_axis=0, concat_axis=2, tiled=True),
        lax.all_to_all(right_side, "ch", split_axis=0, concat_axis=2, tiled=True),
    )
    return (pair_hat, pair_scale, flat_normed, projected, gate_sig, left_half, right_half)


def rear(tri_half, gate_sig, cotangent, layer_out_gain, w_out):
    tri = lax.all_to_all(
        tri_half.astype(jnp.bfloat16), "ch", split_axis=2, concat_axis=0, tiled=True
    ).astype(tri_half.dtype)
    tri_hat, tri_scale = normalize(tri, 0)
    tri_norm = (tri_hat * layer_out_gain[:, None, None]).astype(jnp.bfloat16)
    linear = jnp.einsum("cij,cd->ijd", tri_norm, w_out, preferred_element_type=jnp.float32).reshape(
        -1, w_out.shape[1]
    )
    flat_cot = cotangent.reshape(-1, cotangent.shape[2])
    d_linear = (flat_cot * gate_sig).astype(jnp.bfloat16)
    d_gate = (flat_cot * linear * gate_sig * (1.0 - gate_sig)).astype(jnp.bfloat16)
    d_cube = d_linear.reshape(cotangent.shape[0], cotangent.shape[1], -1)
    d_norm = jnp.einsum("ijd,cd->cij", d_cube, w_out, preferred_element_type=jnp.float32)
    g_out = jnp.einsum("cij,ijd->cd", tri_norm, d_cube, preferred_element_type=jnp.float32)
    tri_grad = norm_back(d_norm * layer_out_gain[:, None, None], tri_hat, tri_scale, 0).astype(
        jnp.bfloat16
    )
    grad_half = lax.all_to_all(tri_grad, "ch", split_axis=0, concat_axis=2, tiled=True)
    return (grad_half, d_gate, g_out)


def front_back(
    cotangent,
    left_half_grad,
    right_half_grad,
    pair_hat,
    pair_scale,
    flat_normed,
    projected,
    d_gate,
    layer_gain,
    w_proj,
    w_gate,
):
    d_left, d_right = (
        lax.all_to_all(
            left_half_grad.astype(jnp.bfloat16), "ch", split_axis=2, concat_axis=0, tiled=True
        ).astype(left_half_grad.dtype),
        lax.all_to_all(
            right_half_grad.astype(jnp.bfloat16), "ch", split_axis=2, concat_axis=0, tiled=True
        ).astype(right_half_grad.dtype),
    )
    width = d_left.shape[0]
    sig_a = jax.nn.sigmoid(projected[:, width : 2 * width])
    sig_b = jax.nn.sigmoid(projected[:, 3 * width :])
    flat_left = d_left.transpose(1, 2, 0).reshape(-1, width)
    flat_right = d_right.transpose(1, 2, 0).reshape(-1, width)
    d_proj = jnp.concatenate(
        [
            flat_left * sig_a,
            flat_left * projected[:, :width] * sig_a * (1.0 - sig_a),
            flat_right * sig_b,
            flat_right * projected[:, 2 * width : 3 * width] * sig_b * (1.0 - sig_b),
        ],
        axis=1,
    ).astype(jnp.bfloat16)
    d_normed = jnp.dot(d_proj, w_proj.T, preferred_element_type=jnp.float32) + jnp.dot(
        d_gate, w_gate.T, preferred_element_type=jnp.float32
    )
    g_proj = jnp.einsum("nc,nd->cd", flat_normed, d_proj, preferred_element_type=jnp.float32)
    g_gate = jnp.einsum("nc,nd->cd", flat_normed, d_gate, preferred_element_type=jnp.float32)
    d_pair = cotangent + norm_back(
        d_normed.reshape(cotangent.shape) * layer_gain, pair_hat, pair_scale, 2
    )
    return (d_pair, g_proj, g_gate)


def outgoing(pair, cotangent, layer_gain, w_proj, w_gate, layer_out_gain, w_out):
    pair_hat, pair_scale, flat_normed, projected, gate_sig, left_half, right_half = front(
        pair, layer_gain, w_proj, w_gate
    )
    tri_half = jnp.einsum(
        "cik,cjk->cij",
        left_half,
        lax.all_gather(right_half, "ax", axis=1, tiled=True),
        preferred_element_type=jnp.float32,
    )
    grad_half, d_gate, g_out = rear(tri_half, gate_sig, cotangent, layer_out_gain, w_out)
    d_left = jnp.einsum(
        "cij,cjk->cik",
        grad_half,
        lax.all_gather(right_half, "ax", axis=1, tiled=True),
        preferred_element_type=jnp.float32,
    )
    turned = lax.all_to_all(grad_half, "ax", split_axis=2, concat_axis=1, tiled=True)
    d_right = jnp.einsum(
        "cij,cik->cjk",
        turned,
        lax.all_gather(left_half, "ax", axis=1, tiled=True),
        preferred_element_type=jnp.float32,
    )
    d_pair, g_proj, g_gate = front_back(
        cotangent,
        d_left,
        d_right,
        pair_hat,
        pair_scale,
        flat_normed,
        projected,
        d_gate,
        layer_gain,
        w_proj,
        w_gate,
    )
    return (d_pair, g_proj, g_gate, g_out)


def incoming(pair, cotangent, layer_gain, w_proj, w_gate, layer_out_gain, w_out):
    pair_hat, pair_scale, flat_normed, projected, gate_sig, left_half, right_half = front(
        pair, layer_gain, w_proj, w_gate
    )
    turned = lax.all_to_all(left_half, "ax", split_axis=2, concat_axis=1, tiled=True)
    part = turned
    tri_half = jnp.einsum(
        "cki,ckj->cij",
        part,
        lax.all_gather(right_half, "ax", axis=1, tiled=True),
        preferred_element_type=jnp.float32,
    )
    grad_half, d_gate, g_out = rear(tri_half, gate_sig, cotangent, layer_out_gain, w_out)
    d_turned = jnp.einsum(
        "ckj,cij->cki",
        lax.all_gather(right_half, "ax", axis=1, tiled=True),
        grad_half,
        preferred_element_type=jnp.float32,
    )
    d_left = lax.all_to_all(
        d_turned.astype(jnp.bfloat16), "ax", split_axis=1, concat_axis=2, tiled=True
    ).astype(d_turned.dtype)
    part = left_half
    d_right = jnp.einsum(
        "cki,cij->ckj",
        part,
        lax.all_gather(grad_half, "ax", axis=1, tiled=True),
        preferred_element_type=jnp.float32,
    )
    d_pair, g_proj, g_gate = front_back(
        cotangent,
        d_left,
        d_right,
        pair_hat,
        pair_scale,
        flat_normed,
        projected,
        d_gate,
        layer_gain,
        w_proj,
        w_gate,
    )
    return (d_pair, g_proj, g_gate, g_out)


def split_crop(
    pair_first, pair_second, grad_out, norm_gain, proj_weight, gate_weight, out_gain, out_weight
):
    count = pair_first.shape[1]
    second = incoming(
        own_cells(pair_second),
        own_cells(grad_out).astype(jnp.float32),
        norm_gain[1],
        proj_weight[1],
        gate_weight[1],
        out_gain[1],
        out_weight[1],
    )
    carried = lax.optimization_barrier(second[0].astype(jnp.bfloat16)).astype(jnp.float32)
    first = outgoing(
        own_cells(pair_first),
        carried,
        norm_gain[0],
        proj_weight[0],
        gate_weight[0],
        out_gain[0],
        out_weight[0],
    )
    totals = lax.psum(
        (
            jnp.stack([first[1], second[1]]),
            jnp.stack([first[2], second[2]]),
            jnp.stack([first[3], second[3]]),
        ),
        ("ax", "ch"),
    )
    grad_in = lax.all_gather(first[0].astype(jnp.bfloat16), "ch", axis=1, tiled=True)
    return (grad_in, totals[0] / count, totals[1] / count, totals[2] / count)


def nt_dot(a, b):
    return lax.dot_general(a, b, (((1,), (1,)), ((), ())), preferred_element_type=jnp.float32)


def tn_dot(a, b):
    return lax.dot_general(a, b, (((0,), (0,)), ((), ())), preferred_element_type=jnp.float32)


def gather_kernel(shares, first_ref, second_ref, cot_ref, held, send_sem, recv_sem):
    me = lax.axis_index("ax")
    barrier = pltpu.get_barrier_semaphore()
    for step in range(1, shares):
        peer = lax.rem(me + step, shares)
        pl.semaphore_signal(
            barrier, inc=1, device_id={"ax": peer}, device_id_type=pl.DeviceIdType.MESH
        )
    held[me, 0] = second_ref[...]
    held[me, 1] = cot_ref[...]
    held[me, 2] = first_ref[...]
    pl.semaphore_wait(barrier, shares - 1)
    copies = []
    for step in range(1, shares):
        peer = lax.rem(me + step, shares)
        copy = pltpu.make_async_remote_copy(
            src_ref=held.at[me],
            dst_ref=held.at[me],
            send_sem=send_sem.at[step],
            recv_sem=recv_sem.at[step],
            device_id={"ax": peer},
            device_id_type=pl.DeviceIdType.MESH,
        )
        copy.start()
        copies.append(copy)
    for copy in copies:
        copy.wait()


def gather_rows(first, second, cot, shares):
    return pl.pallas_call(
        functools.partial(gather_kernel, shares),
        out_shape=jax.ShapeDtypeStruct((shares, 3) + first.shape, first.dtype),
        in_specs=[pl.BlockSpec(memory_space=pltpu.VMEM)] * 3,
        out_specs=pl.BlockSpec(memory_space=pltpu.VMEM),
        scratch_shapes=[
            pltpu.SemaphoreType.DMA((shares,)),
            pltpu.SemaphoreType.DMA((shares,)),
        ],
        compiler_params=pltpu.CompilerParams(collective_id=0, has_side_effects=True),
    )(first, second, cot)


def products(count, out_ref, a_ref, b_ref, a_swapped, b_swapped):
    block = 8
    for start in range(0, count, block):
        sums = [None] * block
        for r in range(count):
            if b_swapped:
                b = b_ref[pl.ds(r, count, stride=count), :]
            else:
                b = b_ref[r * count : (r + 1) * count, :]
            for place in range(block):
                p = start + place
                row = r * count + p if a_swapped else p * count + r
                term = a_ref[row : row + 1, :] * b
                sums[place] = term if sums[place] is None else sums[place] + term
        for place in range(block):
            p = start + place
            out_ref[p * count : (p + 1) * count, :] = sums[place]


def crop_layer(
    layer,
    incoming,
    count,
    pair,
    cot,
    gain_ref,
    proj_ref,
    gate_ref,
    out_gain_ref,
    out_w_ref,
    left_ref,
    right_ref,
    cube_ref,
    d_left_ref,
    d_right_ref,
):
    gain = gain_ref[layer : layer + 1, :]
    out_gain = out_gain_ref[layer : layer + 1, :]
    w_proj = proj_ref[layer]
    w_out = out_w_ref[layer]
    width = w_out.shape[0]
    pair_hat, pair_scale = normalize(pair, 1)
    normed = (pair_hat * gain).astype(jnp.bfloat16)
    projected = jnp.dot(normed, w_proj, preferred_element_type=jnp.float32)
    a_proj = projected[:, :width]
    b_proj = projected[:, 2 * width : 3 * width]
    sig_a = jax.nn.sigmoid(projected[:, width : 2 * width])
    sig_b = jax.nn.sigmoid(projected[:, 3 * width :])
    gate = jax.nn.sigmoid(jnp.dot(normed, gate_ref[layer], preferred_element_type=jnp.float32))
    left_ref[...] = (sig_a * a_proj).astype(jnp.bfloat16).astype(jnp.float32)
    right_ref[...] = (sig_b * b_proj).astype(jnp.bfloat16).astype(jnp.float32)
    if incoming:
        products(count, cube_ref, left_ref, right_ref, True, False)
    else:
        products(count, cube_ref, left_ref, right_ref, False, True)
    tri_hat, tri_scale = normalize(cube_ref[...], 1)
    tri_norm = (tri_hat * out_gain).astype(jnp.bfloat16)
    linear = jnp.dot(tri_norm, w_out, preferred_element_type=jnp.float32)
    scaled = cot * gate
    d_linear = scaled.astype(jnp.bfloat16)
    d_gate = (cot * linear * gate * (1.0 - gate)).astype(jnp.bfloat16)
    h = nt_dot(d_linear, w_out) * out_gain
    cube_ref[...] = (
        norm_back(h, tri_hat, tri_scale, 1).astype(jnp.bfloat16).astype(jnp.float32)
    )
    if incoming:
        products(count, d_left_ref, right_ref, cube_ref, False, True)
        products(count, d_right_ref, left_ref, cube_ref, False, False)
    else:
        products(count, d_left_ref, cube_ref, right_ref, False, False)
        products(count, d_right_ref, cube_ref, left_ref, True, False)
    d_left = d_left_ref[...]
    d_right = d_right_ref[...]
    d_proj = jnp.concatenate(
        [
            (d_left * sig_a).astype(jnp.bfloat16),
            (d_left * a_proj * sig_a * (1.0 - sig_a)).astype(jnp.bfloat16),
            (d_right * sig_b).astype(jnp.bfloat16),
            (d_right * b_proj * sig_b * (1.0 - sig_b)).astype(jnp.bfloat16),
        ],
        axis=1,
    )
    grads = (
        tn_dot(normed, d_proj) / count,
        tn_dot(normed, d_gate) / count,
        tn_dot(tri_norm, d_linear) / count,
    )
    return (d_proj, d_gate, grads)


def pair_back(cot, pair, d_proj, d_gate, gain, w_proj, w_gate):
    pair_hat, pair_scale = normalize(pair, 1)
    d_normed = nt_dot(d_proj, w_proj) + nt_dot(d_gate, w_gate)
    return cot + norm_back(d_normed * gain, pair_hat, pair_scale, 1)


def crop_kernel(
    held,
    gain_ref,
    proj_ref,
    gate_ref,
    out_gain_ref,
    out_w_ref,
    grad_in_ref,
    g_proj_ref,
    g_gate_ref,
    g_out_ref,
    left_ref,
    right_ref,
    cube_ref,
    d_left_ref,
    d_right_ref,
    carried_ref,
    d_proj_ref,
    d_gate_ref,
):
    rows, count, channels = held.shape[2:]
    scratch = (left_ref, right_ref, cube_ref, d_left_ref, d_right_ref)
    weights = (gain_ref, proj_ref, gate_ref, out_gain_ref, out_w_ref)
    second = held[:, 0].reshape(-1, channels).astype(jnp.float32)
    cot = held[:, 1].reshape(-1, channels).astype(jnp.float32)
    d_proj, d_gate, grads = crop_layer(1, True, count, second, cot, *weights, *scratch)
    g_proj_ref[1], g_gate_ref[1], g_out_ref[1] = grads
    carried = pair_back(
        cot, second, d_proj, d_gate, gain_ref[1:2, :], proj_ref[1], gate_ref[1]
    ).astype(jnp.bfloat16)
    carried_ref[...] = carried
    first = held[:, 2].reshape(-1, channels).astype(jnp.float32)
    d_proj, d_gate, grads = crop_layer(
        0, False, count, first, carried.astype(jnp.float32), *weights, *scratch
    )
    g_proj_ref[0], g_gate_ref[0], g_out_ref[0] = grads
    d_proj_ref[...] = d_proj
    d_gate_ref[...] = d_gate
    me = lax.axis_index("ax")
    cells = rows * count
    mine = pl.ds(pl.multiple_of(me * cells, cells), cells)
    d_pair = pair_back(
        carried_ref[mine, :].astype(jnp.float32),
        held[me, 2].reshape(cells, channels).astype(jnp.float32),
        d_proj_ref[mine, :],
        d_gate_ref[mine, :],
        gain_ref[0:1, :],
        proj_ref[0],
        gate_ref[0],
    )
    grad_in_ref[...] = d_pair.astype(jnp.bfloat16).reshape(grad_in_ref.shape)


def whole_crop(
    pair_first, pair_second, grad_out, norm_gain, proj_weight, gate_weight, out_gain, out_weight
):
    shares = lax.axis_size("ax")
    rows, count, channels = pair_first.shape
    held = gather_rows(pair_first, pair_second, grad_out, shares)
    cells = count * count
    width = out_weight.shape[1]
    vmem = pl.BlockSpec(memory_space=pltpu.VMEM)
    f32 = jnp.float32
    return tuple(
        pl.pallas_call(
            crop_kernel,
            out_shape=(
                jax.ShapeDtypeStruct(pair_first.shape, pair_first.dtype),
                jax.ShapeDtypeStruct(proj_weight.shape, f32),
                jax.ShapeDtypeStruct(gate_weight.shape, f32),
                jax.ShapeDtypeStruct(out_weight.shape, f32),
            ),
            in_specs=[vmem] * 6,
            out_specs=(vmem,) * 4,
            scratch_shapes=[
                pltpu.VMEM((cells, width), f32),
                pltpu.VMEM((cells, width), f32),
                pltpu.VMEM((cells, width), f32),
                pltpu.VMEM((cells, width), f32),
                pltpu.VMEM((cells, width), f32),
                pltpu.VMEM((cells, channels), jnp.bfloat16),
                pltpu.VMEM((cells, 4 * width), jnp.bfloat16),
                pltpu.VMEM((cells, channels), jnp.bfloat16),
            ],
            compiler_params=pltpu.CompilerParams(vmem_limit_bytes=32 * 1024 * 1024),
        )(held, norm_gain, proj_weight, gate_weight, out_gain, out_weight)
    )


def on_device(*args):
    count = args[0].shape[1]
    if count % 16 == 0 and count <= 32:
        return whole_crop(*args)
    return split_crop(*args)


def solution(mesh):
    placed = (
        P(("grp", "ax"), None, None),
        P(("grp", "ax"), None, None),
        P(("grp", "ax"), None, None),
        P(),
        P(),
        P(),
        P(),
        P(),
    )
    return jax.shard_map(
        on_device,
        mesh=mesh,
        in_specs=placed,
        out_specs=(
            P(("grp", "ax"), None, None),
            P("grp", None, None),
            P("grp", None, None),
            P("grp", None, None),
        ),
        check_vma=False,
    )
```

```python
import functools

import jax
import jax.numpy as jnp
from jax import lax
from jax.experimental import pallas as pl
from jax.experimental.pallas import tpu as pltpu
from jax.sharding import PartitionSpec as P

EPS = 1e-05


def normalize(values, axis):
    center = values - jnp.mean(values, axis=axis, keepdims=True)
    scale = lax.rsqrt(jnp.mean(center * center, axis=axis, keepdims=True) + EPS)
    return (center * scale, scale)


def norm_back(grad, normed, scale, axis):
    return scale * (
        grad
        - jnp.mean(grad, axis=axis, keepdims=True)
        - normed * jnp.mean(grad * normed, axis=axis, keepdims=True)
    )


def own_cells(values):
    share = values.shape[1] // lax.axis_size("ch")
    return lax.dynamic_slice_in_dim(values, lax.axis_index("ch") * share, share, 1)


def front(pair, layer_gain, w_proj, w_gate):
    width = w_proj.shape[1] // 4
    rows = pair.shape[0]
    count = pair.shape[1]
    pair_hat, pair_scale = normalize(pair.astype(jnp.float32), 2)
    flat_normed = (pair_hat * layer_gain).astype(jnp.bfloat16).reshape(-1, pair.shape[2])
    projected = jnp.dot(flat_normed, w_proj, preferred_element_type=jnp.float32)
    gate_sig = jax.nn.sigmoid(jnp.dot(flat_normed, w_gate, preferred_element_type=jnp.float32))
    sig_a = jax.nn.sigmoid(projected[:, width : 2 * width])
    sig_b = jax.nn.sigmoid(projected[:, 3 * width :])
    left_side = (
        (sig_a * projected[:, :width])
        .astype(jnp.bfloat16)
        .reshape(rows, count, width)
        .transpose(2, 0, 1)
    )
    right_side = (
        (sig_b * projected[:, 2 * width : 3 * width])
        .astype(jnp.bfloat16)
        .reshape(rows, count, width)
        .transpose(2, 0, 1)
    )
    left_half, right_half = (
        lax.all_to_all(left_side, "ch", split_axis=0, concat_axis=2, tiled=True),
        lax.all_to_all(right_side, "ch", split_axis=0, concat_axis=2, tiled=True),
    )
    return (pair_hat, pair_scale, flat_normed, projected, gate_sig, left_half, right_half)


def rear(tri_half, gate_sig, cotangent, layer_out_gain, w_out):
    tri = lax.all_to_all(
        tri_half.astype(jnp.bfloat16), "ch", split_axis=2, concat_axis=0, tiled=True
    ).astype(tri_half.dtype)
    tri_hat, tri_scale = normalize(tri, 0)
    tri_norm = (tri_hat * layer_out_gain[:, None, None]).astype(jnp.bfloat16)
    linear = jnp.einsum("cij,cd->ijd", tri_norm, w_out, preferred_element_type=jnp.float32).reshape(
        -1, w_out.shape[1]
    )
    flat_cot = cotangent.reshape(-1, cotangent.shape[2])
    d_linear = (flat_cot * gate_sig).astype(jnp.bfloat16)
    d_gate = (flat_cot * linear * gate_sig * (1.0 - gate_sig)).astype(jnp.bfloat16)
    d_cube = d_linear.reshape(cotangent.shape[0], cotangent.shape[1], -1)
    d_norm = jnp.einsum("ijd,cd->cij", d_cube, w_out, preferred_element_type=jnp.float32)
    g_out = jnp.einsum("cij,ijd->cd", tri_norm, d_cube, preferred_element_type=jnp.float32)
    tri_grad = norm_back(d_norm * layer_out_gain[:, None, None], tri_hat, tri_scale, 0).astype(
        jnp.bfloat16
    )
    grad_half = lax.all_to_all(tri_grad, "ch", split_axis=0, concat_axis=2, tiled=True)
    return (grad_half, d_gate, g_out)


def front_back(
    cotangent,
    left_half_grad,
    right_half_grad,
    pair_hat,
    pair_scale,
    flat_normed,
    projected,
    d_gate,
    layer_gain,
    w_proj,
    w_gate,
):
    d_left, d_right = (
        lax.all_to_all(
            left_half_grad.astype(jnp.bfloat16), "ch", split_axis=2, concat_axis=0, tiled=True
        ).astype(left_half_grad.dtype),
        lax.all_to_all(
            right_half_grad.astype(jnp.bfloat16), "ch", split_axis=2, concat_axis=0, tiled=True
        ).astype(right_half_grad.dtype),
    )
    width = d_left.shape[0]
    sig_a = jax.nn.sigmoid(projected[:, width : 2 * width])
    sig_b = jax.nn.sigmoid(projected[:, 3 * width :])
    flat_left = d_left.transpose(1, 2, 0).reshape(-1, width)
    flat_right = d_right.transpose(1, 2, 0).reshape(-1, width)
    d_proj = jnp.concatenate(
        [
            flat_left * sig_a,
            flat_left * projected[:, :width] * sig_a * (1.0 - sig_a),
            flat_right * sig_b,
            flat_right * projected[:, 2 * width : 3 * width] * sig_b * (1.0 - sig_b),
        ],
        axis=1,
    ).astype(jnp.bfloat16)
    d_normed = jnp.dot(d_proj, w_proj.T, preferred_element_type=jnp.float32) + jnp.dot(
        d_gate, w_gate.T, preferred_element_type=jnp.float32
    )
    g_proj = jnp.einsum("nc,nd->cd", flat_normed, d_proj, preferred_element_type=jnp.float32)
    g_gate = jnp.einsum("nc,nd->cd", flat_normed, d_gate, preferred_element_type=jnp.float32)
    d_pair = cotangent + norm_back(
        d_normed.reshape(cotangent.shape) * layer_gain, pair_hat, pair_scale, 2
    )
    return (d_pair, g_proj, g_gate)


def outgoing(pair, cotangent, layer_gain, w_proj, w_gate, layer_out_gain, w_out):
    pair_hat, pair_scale, flat_normed, projected, gate_sig, left_half, right_half = front(
        pair, layer_gain, w_proj, w_gate
    )
    tri_half = jnp.einsum(
        "cik,cjk->cij",
        left_half,
        lax.all_gather(right_half, "ax", axis=1, tiled=True),
        preferred_element_type=jnp.float32,
    )
    grad_half, d_gate, g_out = rear(tri_half, gate_sig, cotangent, layer_out_gain, w_out)
    d_left = jnp.einsum(
        "cij,cjk->cik",
        grad_half,
        lax.all_gather(right_half, "ax", axis=1, tiled=True),
        preferred_element_type=jnp.float32,
    )
    turned = lax.all_to_all(grad_half, "ax", split_axis=2, concat_axis=1, tiled=True)
    d_right = jnp.einsum(
        "cij,cik->cjk",
        turned,
        lax.all_gather(left_half, "ax", axis=1, tiled=True),
        preferred_element_type=jnp.float32,
    )
    d_pair, g_proj, g_gate = front_back(
        cotangent,
        d_left,
        d_right,
        pair_hat,
        pair_scale,
        flat_normed,
        projected,
        d_gate,
        layer_gain,
        w_proj,
        w_gate,
    )
    return (d_pair, g_proj, g_gate, g_out)


def incoming(pair, cotangent, layer_gain, w_proj, w_gate, layer_out_gain, w_out):
    pair_hat, pair_scale, flat_normed, projected, gate_sig, left_half, right_half = front(
        pair, layer_gain, w_proj, w_gate
    )
    turned = lax.all_to_all(left_half, "ax", split_axis=2, concat_axis=1, tiled=True)
    part = turned
    tri_half = jnp.einsum(
        "cki,ckj->cij",
        part,
        lax.all_gather(right_half, "ax", axis=1, tiled=True),
        preferred_element_type=jnp.float32,
    )
    grad_half, d_gate, g_out = rear(tri_half, gate_sig, cotangent, layer_out_gain, w_out)
    d_turned = jnp.einsum(
        "ckj,cij->cki",
        lax.all_gather(right_half, "ax", axis=1, tiled=True),
        grad_half,
        preferred_element_type=jnp.float32,
    )
    d_left = lax.all_to_all(
        d_turned.astype(jnp.bfloat16), "ax", split_axis=1, concat_axis=2, tiled=True
    ).astype(d_turned.dtype)
    part = left_half
    d_right = jnp.einsum(
        "cki,cij->ckj",
        part,
        lax.all_gather(grad_half, "ax", axis=1, tiled=True),
        preferred_element_type=jnp.float32,
    )
    d_pair, g_proj, g_gate = front_back(
        cotangent,
        d_left,
        d_right,
        pair_hat,
        pair_scale,
        flat_normed,
        projected,
        d_gate,
        layer_gain,
        w_proj,
        w_gate,
    )
    return (d_pair, g_proj, g_gate, g_out)


def split_crop(
    pair_first, pair_second, grad_out, norm_gain, proj_weight, gate_weight, out_gain, out_weight
):
    count = pair_first.shape[1]
    second = incoming(
        own_cells(pair_second),
        own_cells(grad_out).astype(jnp.float32),
        norm_gain[1],
        proj_weight[1],
        gate_weight[1],
        out_gain[1],
        out_weight[1],
    )
    carried = lax.optimization_barrier(second[0].astype(jnp.bfloat16)).astype(jnp.float32)
    first = outgoing(
        own_cells(pair_first),
        carried,
        norm_gain[0],
        proj_weight[0],
        gate_weight[0],
        out_gain[0],
        out_weight[0],
    )
    totals = lax.psum(
        (
            jnp.stack([first[1], second[1]]),
            jnp.stack([first[2], second[2]]),
            jnp.stack([first[3], second[3]]),
        ),
        ("ax", "ch"),
    )
    grad_in = lax.all_gather(first[0].astype(jnp.bfloat16), "ch", axis=1, tiled=True)
    return (grad_in, totals[0] / count, totals[1] / count, totals[2] / count)


def nt_dot(a, b):
    return lax.dot_general(a, b, (((1,), (1,)), ((), ())), preferred_element_type=jnp.float32)


def tn_dot(a, b):
    return lax.dot_general(a, b, (((0,), (0,)), ((), ())), preferred_element_type=jnp.float32)


def gather_kernel(shares, halves, first_ref, second_ref, cot_ref, *rest):
    weight_refs, held, weight_outs = rest[:5], rest[5], rest[6:11]
    stage_sem, weight_sem, send_sem, recv_sem, pass_sem, got_sem = rest[11:]
    me = lax.axis_index("ax")
    core = lax.axis_index("ch")
    part = held.shape[3]
    mesh_id = pl.DeviceIdType.MESH
    near_first = sorted(range(1, shares), key=lambda step: min(step, shares - step))
    barrier = pltpu.get_barrier_semaphore()
    for step in reversed(near_first):
        peer = lax.rem(me + step, shares)
        pl.semaphore_signal(barrier, inc=1, device_id={"ax": peer}, device_id_type=mesh_id)
    for turn in range(1, halves):
        mate = lax.rem(core + turn, halves)
        pl.semaphore_signal(barrier, inc=1, device_id={"ch": mate}, device_id_type=mesh_id)
    staged = []
    for place, ref in enumerate((second_ref, cot_ref, first_ref)):
        for half in range(halves):
            copy = pltpu.make_async_copy(
                ref.at[pl.ds(half * part, part)],
                held.at[me, half, place],
                stage_sem.at[place, half],
            )
            copy.start()
            staged.append(copy)
    loads = [
        pltpu.make_async_copy(ref, out, weight_sem.at[place])
        for place, (ref, out) in enumerate(zip(weight_refs, weight_outs))
    ]
    for copy in loads:
        copy.start()
    for copy in staged:
        copy.wait()
    pl.semaphore_wait(barrier, shares + halves - 2)
    sends = {}
    for step in reversed(near_first):
        peer = lax.rem(me + step, shares)
        sends[step] = pltpu.make_async_remote_copy(
            src_ref=held.at[me, core],
            dst_ref=held.at[me, core],
            send_sem=send_sem.at[step],
            recv_sem=recv_sem.at[step],
            device_id={"ax": peer},
            device_id_type=mesh_id,
        )
        sends[step].start()
    passes = []
    for step in near_first:
        source = lax.rem(me - step + shares, shares)
        sends[step].wait_recv()
        for turn in range(1, halves):
            mate = lax.rem(core + turn, halves)
            copy = pltpu.make_async_remote_copy(
                src_ref=held.at[source, core],
                dst_ref=held.at[source, core],
                send_sem=pass_sem.at[step, turn],
                recv_sem=got_sem.at[step, turn],
                device_id={"ch": mate},
                device_id_type=mesh_id,
            )
            copy.start()
            passes.append(copy)
    for copy in passes:
        copy.wait_recv()
    for step in near_first:
        sends[step].wait_send()
    for copy in passes:
        copy.wait_send()
    for copy in loads:
        copy.wait()


def gather_rows(first, second, cot, weights, shares, halves):
    rows, count, channels = first.shape
    shape = (shares, halves, 3, rows // halves, count, channels)
    hbm = pl.BlockSpec(memory_space=pltpu.HBM)
    vmem = pl.BlockSpec(memory_space=pltpu.VMEM)
    return pl.pallas_call(
        functools.partial(gather_kernel, shares, halves),
        out_shape=(
            pltpu.VMEM(shape, first.dtype),
            *(pltpu.VMEM(weight.shape, weight.dtype) for weight in weights),
        ),
        in_specs=[hbm] * 8,
        out_specs=(vmem,) * 6,
        scratch_shapes=[
            pltpu.SemaphoreType.DMA((3, halves)),
            pltpu.SemaphoreType.DMA((5,)),
            pltpu.SemaphoreType.DMA((shares,)),
            pltpu.SemaphoreType.DMA((shares,)),
            pltpu.SemaphoreType.DMA((shares, halves)),
            pltpu.SemaphoreType.DMA((shares, halves)),
        ],
        compiler_params=pltpu.CompilerParams(
            collective_id=0, has_side_effects=True, vmem_limit_bytes=4 * 1024 * 1024
        ),
    )(*(pltpu.with_memory_space_constraint(x, pltpu.HBM) for x in (first, second, cot, *weights)))


def products(count, out_ref, a_ref, b_ref, a_swapped, b_swapped):
    block = 8
    for start in range(0, count, block):
        sums = [None] * block
        for r in range(count):
            if b_swapped:
                b = b_ref[pl.ds(r, count, stride=count), :]
            else:
                b = b_ref[r * count : (r + 1) * count, :]
            for place in range(block):
                p = start + place
                row = r * count + p if a_swapped else p * count + r
                term = a_ref[row : row + 1, :] * b
                sums[place] = term if sums[place] is None else sums[place] + term
        for place in range(block):
            p = start + place
            out_ref[p * count : (p + 1) * count, :] = sums[place]


def crop_layer(
    layer,
    incoming,
    count,
    pair,
    cot,
    gain_ref,
    proj_ref,
    gate_ref,
    out_gain_ref,
    out_w_ref,
    left_ref,
    right_ref,
    cube_ref,
    d_left_ref,
    d_right_ref,
):
    gain = gain_ref[layer : layer + 1, :]
    out_gain = out_gain_ref[layer : layer + 1, :]
    w_proj = proj_ref[layer]
    w_out = out_w_ref[layer]
    width = w_out.shape[0]
    pair_hat, pair_scale = normalize(pair, 1)
    normed = (pair_hat * gain).astype(jnp.bfloat16)
    projected = jnp.dot(normed, w_proj, preferred_element_type=jnp.float32)
    a_proj = projected[:, :width]
    b_proj = projected[:, 2 * width : 3 * width]
    sig_a = jax.nn.sigmoid(projected[:, width : 2 * width])
    sig_b = jax.nn.sigmoid(projected[:, 3 * width :])
    gate = jax.nn.sigmoid(jnp.dot(normed, gate_ref[layer], preferred_element_type=jnp.float32))
    left_ref[...] = (sig_a * a_proj).astype(jnp.bfloat16).astype(jnp.float32)
    right_ref[...] = (sig_b * b_proj).astype(jnp.bfloat16).astype(jnp.float32)
    if incoming:
        products(count, cube_ref, left_ref, right_ref, True, False)
    else:
        products(count, cube_ref, left_ref, right_ref, False, True)
    tri_hat, tri_scale = normalize(cube_ref[...], 1)
    tri_norm = (tri_hat * out_gain).astype(jnp.bfloat16)
    linear = jnp.dot(tri_norm, w_out, preferred_element_type=jnp.float32)
    scaled = cot * gate
    d_linear = scaled.astype(jnp.bfloat16)
    d_gate = (cot * linear * gate * (1.0 - gate)).astype(jnp.bfloat16)
    h = nt_dot(d_linear, w_out) * out_gain
    cube_ref[...] = (
        norm_back(h, tri_hat, tri_scale, 1).astype(jnp.bfloat16).astype(jnp.float32)
    )
    if incoming:
        products(count, d_left_ref, right_ref, cube_ref, False, True)
        products(count, d_right_ref, left_ref, cube_ref, False, False)
    else:
        products(count, d_left_ref, cube_ref, right_ref, False, False)
        products(count, d_right_ref, cube_ref, left_ref, True, False)
    d_left = d_left_ref[...]
    d_right = d_right_ref[...]
    d_proj = jnp.concatenate(
        [
            (d_left * sig_a).astype(jnp.bfloat16),
            (d_left * a_proj * sig_a * (1.0 - sig_a)).astype(jnp.bfloat16),
            (d_right * sig_b).astype(jnp.bfloat16),
            (d_right * b_proj * sig_b * (1.0 - sig_b)).astype(jnp.bfloat16),
        ],
        axis=1,
    )
    grads = (
        tn_dot(normed, d_proj) / count,
        tn_dot(normed, d_gate) / count,
        tn_dot(tri_norm, d_linear) / count,
    )
    return (d_proj, d_gate, grads)


def pair_back(cot, pair, d_proj, d_gate, gain, w_proj, w_gate):
    pair_hat, pair_scale = normalize(pair, 1)
    d_normed = nt_dot(d_proj, w_proj) + nt_dot(d_gate, w_gate)
    return cot + norm_back(d_normed * gain, pair_hat, pair_scale, 1)


def crop_kernel(
    held,
    gain_ref,
    proj_ref,
    gate_ref,
    out_gain_ref,
    out_w_ref,
    grad_in_ref,
    g_proj_ref,
    g_gate_ref,
    g_out_ref,
    left_ref,
    right_ref,
    cube_ref,
    d_left_ref,
    d_right_ref,
    carried_ref,
    d_proj_ref,
    d_gate_ref,
):
    count, channels = held.shape[4:]
    rows = held.shape[1] * held.shape[3]
    scratch = (left_ref, right_ref, cube_ref, d_left_ref, d_right_ref)
    weights = (gain_ref, proj_ref, gate_ref, out_gain_ref, out_w_ref)
    second = held[:, :, 0].reshape(-1, channels).astype(jnp.float32)
    cot = held[:, :, 1].reshape(-1, channels).astype(jnp.float32)
    d_proj, d_gate, grads = crop_layer(1, True, count, second, cot, *weights, *scratch)
    g_proj_ref[1], g_gate_ref[1], g_out_ref[1] = grads
    carried = pair_back(
        cot, second, d_proj, d_gate, gain_ref[1:2, :], proj_ref[1], gate_ref[1]
    ).astype(jnp.bfloat16)
    carried_ref[...] = carried
    first = held[:, :, 2].reshape(-1, channels).astype(jnp.float32)
    d_proj, d_gate, grads = crop_layer(
        0, False, count, first, carried.astype(jnp.float32), *weights, *scratch
    )
    g_proj_ref[0], g_gate_ref[0], g_out_ref[0] = grads
    d_proj_ref[...] = d_proj
    d_gate_ref[...] = d_gate
    me = lax.axis_index("ax")
    cells = rows * count
    mine = pl.ds(pl.multiple_of(me * cells, cells), cells)
    d_pair = pair_back(
        carried_ref[mine, :].astype(jnp.float32),
        held[me, :, 2].reshape(cells, channels).astype(jnp.float32),
        d_proj_ref[mine, :],
        d_gate_ref[mine, :],
        gain_ref[0:1, :],
        proj_ref[0],
        gate_ref[0],
    )
    grad_in_ref[...] = d_pair.astype(jnp.bfloat16).reshape(grad_in_ref.shape)


def whole_crop(
    pair_first, pair_second, grad_out, norm_gain, proj_weight, gate_weight, out_gain, out_weight
):
    shares = lax.axis_size("ax")
    rows, count, channels = pair_first.shape
    weights = (norm_gain, proj_weight, gate_weight, out_gain, out_weight)
    placed = gather_rows(
        pair_first, pair_second, grad_out, weights, shares, lax.axis_size("ch")
    )
    cells = count * count
    width = out_weight.shape[1]
    vmem = pl.BlockSpec(memory_space=pltpu.VMEM)
    f32 = jnp.float32
    return tuple(
        pl.pallas_call(
            crop_kernel,
            out_shape=(
                jax.ShapeDtypeStruct(pair_first.shape, pair_first.dtype),
                jax.ShapeDtypeStruct(proj_weight.shape, f32),
                jax.ShapeDtypeStruct(gate_weight.shape, f32),
                jax.ShapeDtypeStruct(out_weight.shape, f32),
            ),
            in_specs=[vmem] * 6,
            out_specs=(vmem,) * 4,
            scratch_shapes=[
                pltpu.VMEM((cells, width), f32),
                pltpu.VMEM((cells, width), f32),
                pltpu.VMEM((cells, width), f32),
                pltpu.VMEM((cells, width), f32),
                pltpu.VMEM((cells, width), f32),
                pltpu.VMEM((cells, channels), jnp.bfloat16),
                pltpu.VMEM((cells, 4 * width), jnp.bfloat16),
                pltpu.VMEM((cells, channels), jnp.bfloat16),
            ],
            compiler_params=pltpu.CompilerParams(vmem_limit_bytes=16 * 1024 * 1024),
        )(*placed)
    )


def on_device(*args):
    rows, count = args[0].shape[:2]
    if count % 16 == 0 and count <= 32 and rows % lax.axis_size("ch") == 0:
        return whole_crop(*args)
    return split_crop(*args)


def solution(mesh):
    placed = (
        P(("grp", "ax"), None, None),
        P(("grp", "ax"), None, None),
        P(("grp", "ax"), None, None),
        P(),
        P(),
        P(),
        P(),
        P(),
    )
    return jax.shard_map(
        on_device,
        mesh=mesh,
        in_specs=placed,
        out_specs=(
            P(("grp", "ax"), None, None),
            P("grp", None, None),
            P("grp", None, None),
            P("grp", None, None),
        ),
        check_vma=False,
    )
```

```python
import functools

import jax
import jax.numpy as jnp
from jax import lax
from jax.experimental import pallas as pl
from jax.experimental.pallas import tpu as pltpu
from jax.sharding import PartitionSpec as P

EPS = 1e-05


def normalize(values, axis):
    center = values - jnp.mean(values, axis=axis, keepdims=True)
    scale = lax.rsqrt(jnp.mean(center * center, axis=axis, keepdims=True) + EPS)
    return (center * scale, scale)


def norm_back(grad, normed, scale, axis):
    return scale * (
        grad
        - jnp.mean(grad, axis=axis, keepdims=True)
        - normed * jnp.mean(grad * normed, axis=axis, keepdims=True)
    )


def own_cells(values):
    share = values.shape[1] // lax.axis_size("ch")
    return lax.dynamic_slice_in_dim(values, lax.axis_index("ch") * share, share, 1)


def front(pair, layer_gain, w_proj, w_gate):
    width = w_proj.shape[1] // 4
    rows = pair.shape[0]
    count = pair.shape[1]
    pair_hat, pair_scale = normalize(pair.astype(jnp.float32), 2)
    flat_normed = (pair_hat * layer_gain).astype(jnp.bfloat16).reshape(-1, pair.shape[2])
    projected = jnp.dot(flat_normed, w_proj, preferred_element_type=jnp.float32)
    gate_sig = jax.nn.sigmoid(jnp.dot(flat_normed, w_gate, preferred_element_type=jnp.float32))
    sig_a = jax.nn.sigmoid(projected[:, width : 2 * width])
    sig_b = jax.nn.sigmoid(projected[:, 3 * width :])
    left_side = (
        (sig_a * projected[:, :width])
        .astype(jnp.bfloat16)
        .reshape(rows, count, width)
        .transpose(2, 0, 1)
    )
    right_side = (
        (sig_b * projected[:, 2 * width : 3 * width])
        .astype(jnp.bfloat16)
        .reshape(rows, count, width)
        .transpose(2, 0, 1)
    )
    left_half, right_half = (
        lax.all_to_all(left_side, "ch", split_axis=0, concat_axis=2, tiled=True),
        lax.all_to_all(right_side, "ch", split_axis=0, concat_axis=2, tiled=True),
    )
    return (pair_hat, pair_scale, flat_normed, projected, gate_sig, left_half, right_half)


def rear(tri_half, gate_sig, cotangent, layer_out_gain, w_out):
    tri = lax.all_to_all(
        tri_half.astype(jnp.bfloat16), "ch", split_axis=2, concat_axis=0, tiled=True
    ).astype(tri_half.dtype)
    tri_hat, tri_scale = normalize(tri, 0)
    tri_norm = (tri_hat * layer_out_gain[:, None, None]).astype(jnp.bfloat16)
    linear = jnp.einsum("cij,cd->ijd", tri_norm, w_out, preferred_element_type=jnp.float32).reshape(
        -1, w_out.shape[1]
    )
    flat_cot = cotangent.reshape(-1, cotangent.shape[2])
    d_linear = (flat_cot * gate_sig).astype(jnp.bfloat16)
    d_gate = (flat_cot * linear * gate_sig * (1.0 - gate_sig)).astype(jnp.bfloat16)
    d_cube = d_linear.reshape(cotangent.shape[0], cotangent.shape[1], -1)
    d_norm = jnp.einsum("ijd,cd->cij", d_cube, w_out, preferred_element_type=jnp.float32)
    g_out = jnp.einsum("cij,ijd->cd", tri_norm, d_cube, preferred_element_type=jnp.float32)
    tri_grad = norm_back(d_norm * layer_out_gain[:, None, None], tri_hat, tri_scale, 0).astype(
        jnp.bfloat16
    )
    grad_half = lax.all_to_all(tri_grad, "ch", split_axis=0, concat_axis=2, tiled=True)
    return (grad_half, d_gate, g_out)


def front_back(
    cotangent,
    left_half_grad,
    right_half_grad,
    pair_hat,
    pair_scale,
    flat_normed,
    projected,
    d_gate,
    layer_gain,
    w_proj,
    w_gate,
):
    d_left, d_right = (
        lax.all_to_all(
            left_half_grad.astype(jnp.bfloat16), "ch", split_axis=2, concat_axis=0, tiled=True
        ).astype(left_half_grad.dtype),
        lax.all_to_all(
            right_half_grad.astype(jnp.bfloat16), "ch", split_axis=2, concat_axis=0, tiled=True
        ).astype(right_half_grad.dtype),
    )
    width = d_left.shape[0]
    sig_a = jax.nn.sigmoid(projected[:, width : 2 * width])
    sig_b = jax.nn.sigmoid(projected[:, 3 * width :])
    flat_left = d_left.transpose(1, 2, 0).reshape(-1, width)
    flat_right = d_right.transpose(1, 2, 0).reshape(-1, width)
    d_proj = jnp.concatenate(
        [
            flat_left * sig_a,
            flat_left * projected[:, :width] * sig_a * (1.0 - sig_a),
            flat_right * sig_b,
            flat_right * projected[:, 2 * width : 3 * width] * sig_b * (1.0 - sig_b),
        ],
        axis=1,
    ).astype(jnp.bfloat16)
    d_normed = jnp.dot(d_proj, w_proj.T, preferred_element_type=jnp.float32) + jnp.dot(
        d_gate, w_gate.T, preferred_element_type=jnp.float32
    )
    g_proj = jnp.einsum("nc,nd->cd", flat_normed, d_proj, preferred_element_type=jnp.float32)
    g_gate = jnp.einsum("nc,nd->cd", flat_normed, d_gate, preferred_element_type=jnp.float32)
    d_pair = cotangent + norm_back(
        d_normed.reshape(cotangent.shape) * layer_gain, pair_hat, pair_scale, 2
    )
    return (d_pair, g_proj, g_gate)


def outgoing(pair, cotangent, layer_gain, w_proj, w_gate, layer_out_gain, w_out):
    pair_hat, pair_scale, flat_normed, projected, gate_sig, left_half, right_half = front(
        pair, layer_gain, w_proj, w_gate
    )
    tri_half = jnp.einsum(
        "cik,cjk->cij",
        left_half,
        lax.all_gather(right_half, "ax", axis=1, tiled=True),
        preferred_element_type=jnp.float32,
    )
    grad_half, d_gate, g_out = rear(tri_half, gate_sig, cotangent, layer_out_gain, w_out)
    d_left = jnp.einsum(
        "cij,cjk->cik",
        grad_half,
        lax.all_gather(right_half, "ax", axis=1, tiled=True),
        preferred_element_type=jnp.float32,
    )
    turned = lax.all_to_all(grad_half, "ax", split_axis=2, concat_axis=1, tiled=True)
    d_right = jnp.einsum(
        "cij,cik->cjk",
        turned,
        lax.all_gather(left_half, "ax", axis=1, tiled=True),
        preferred_element_type=jnp.float32,
    )
    d_pair, g_proj, g_gate = front_back(
        cotangent,
        d_left,
        d_right,
        pair_hat,
        pair_scale,
        flat_normed,
        projected,
        d_gate,
        layer_gain,
        w_proj,
        w_gate,
    )
    return (d_pair, g_proj, g_gate, g_out)


def incoming(pair, cotangent, layer_gain, w_proj, w_gate, layer_out_gain, w_out):
    pair_hat, pair_scale, flat_normed, projected, gate_sig, left_half, right_half = front(
        pair, layer_gain, w_proj, w_gate
    )
    turned = lax.all_to_all(left_half, "ax", split_axis=2, concat_axis=1, tiled=True)
    part = turned
    tri_half = jnp.einsum(
        "cki,ckj->cij",
        part,
        lax.all_gather(right_half, "ax", axis=1, tiled=True),
        preferred_element_type=jnp.float32,
    )
    grad_half, d_gate, g_out = rear(tri_half, gate_sig, cotangent, layer_out_gain, w_out)
    d_turned = jnp.einsum(
        "ckj,cij->cki",
        lax.all_gather(right_half, "ax", axis=1, tiled=True),
        grad_half,
        preferred_element_type=jnp.float32,
    )
    d_left = lax.all_to_all(
        d_turned.astype(jnp.bfloat16), "ax", split_axis=1, concat_axis=2, tiled=True
    ).astype(d_turned.dtype)
    part = left_half
    d_right = jnp.einsum(
        "cki,cij->ckj",
        part,
        lax.all_gather(grad_half, "ax", axis=1, tiled=True),
        preferred_element_type=jnp.float32,
    )
    d_pair, g_proj, g_gate = front_back(
        cotangent,
        d_left,
        d_right,
        pair_hat,
        pair_scale,
        flat_normed,
        projected,
        d_gate,
        layer_gain,
        w_proj,
        w_gate,
    )
    return (d_pair, g_proj, g_gate, g_out)


def split_crop(
    pair_first, pair_second, grad_out, norm_gain, proj_weight, gate_weight, out_gain, out_weight
):
    count = pair_first.shape[1]
    second = incoming(
        own_cells(pair_second),
        own_cells(grad_out).astype(jnp.float32),
        norm_gain[1],
        proj_weight[1],
        gate_weight[1],
        out_gain[1],
        out_weight[1],
    )
    carried = lax.optimization_barrier(second[0].astype(jnp.bfloat16)).astype(jnp.float32)
    first = outgoing(
        own_cells(pair_first),
        carried,
        norm_gain[0],
        proj_weight[0],
        gate_weight[0],
        out_gain[0],
        out_weight[0],
    )
    totals = lax.psum(
        (
            jnp.stack([first[1], second[1]]),
            jnp.stack([first[2], second[2]]),
            jnp.stack([first[3], second[3]]),
        ),
        ("ax", "ch"),
    )
    grad_in = lax.all_gather(first[0].astype(jnp.bfloat16), "ch", axis=1, tiled=True)
    return (grad_in, totals[0] / count, totals[1] / count, totals[2] / count)


def nt_dot(a, b):
    return lax.dot_general(a, b, (((1,), (1,)), ((), ())), preferred_element_type=jnp.float32)


def tn_dot(a, b):
    return lax.dot_general(a, b, (((0,), (0,)), ((), ())), preferred_element_type=jnp.float32)


def products(count, out_ref, a_ref, b_ref, a_swapped, b_swapped):
    block = 8
    for start in range(0, count, block):
        sums = [None] * block
        for r in range(count):
            if b_swapped:
                b = b_ref[pl.ds(r, count, stride=count), :]
            else:
                b = b_ref[r * count : (r + 1) * count, :]
            for place in range(block):
                p = start + place
                row = r * count + p if a_swapped else p * count + r
                term = a_ref[row : row + 1, :] * b
                sums[place] = term if sums[place] is None else sums[place] + term
        for place in range(block):
            p = start + place
            out_ref[p * count : (p + 1) * count, :] = sums[place]


def crop_layer(
    layer,
    incoming,
    count,
    pair,
    fetch_cot,
    gain_ref,
    proj_ref,
    gate_ref,
    out_gain_ref,
    out_w_ref,
    left_ref,
    right_ref,
    cube_ref,
    d_left_ref,
    d_right_ref,
):
    gain = gain_ref[layer : layer + 1, :]
    out_gain = out_gain_ref[layer : layer + 1, :]
    w_proj = proj_ref[layer]
    w_out = out_w_ref[layer]
    width = w_out.shape[0]
    pair_hat, pair_scale = normalize(pair, 1)
    normed = (pair_hat * gain).astype(jnp.bfloat16)
    projected = jnp.dot(normed, w_proj, preferred_element_type=jnp.float32)
    a_proj = projected[:, :width]
    b_proj = projected[:, 2 * width : 3 * width]
    sig_a = jax.nn.sigmoid(projected[:, width : 2 * width])
    sig_b = jax.nn.sigmoid(projected[:, 3 * width :])
    gate = jax.nn.sigmoid(jnp.dot(normed, gate_ref[layer], preferred_element_type=jnp.float32))
    left_ref[...] = (sig_a * a_proj).astype(jnp.bfloat16).astype(jnp.float32)
    right_ref[...] = (sig_b * b_proj).astype(jnp.bfloat16).astype(jnp.float32)
    if incoming:
        products(count, cube_ref, left_ref, right_ref, True, False)
    else:
        products(count, cube_ref, left_ref, right_ref, False, True)
    tri_hat, tri_scale = normalize(cube_ref[...], 1)
    tri_norm = (tri_hat * out_gain).astype(jnp.bfloat16)
    linear = jnp.dot(tri_norm, w_out, preferred_element_type=jnp.float32)
    cot = fetch_cot()
    scaled = cot * gate
    d_linear = scaled.astype(jnp.bfloat16)
    d_gate = (cot * linear * gate * (1.0 - gate)).astype(jnp.bfloat16)
    h = nt_dot(d_linear, w_out) * out_gain
    cube_ref[...] = (
        norm_back(h, tri_hat, tri_scale, 1).astype(jnp.bfloat16).astype(jnp.float32)
    )
    if incoming:
        products(count, d_left_ref, right_ref, cube_ref, False, True)
        products(count, d_right_ref, left_ref, cube_ref, False, False)
    else:
        products(count, d_left_ref, cube_ref, right_ref, False, False)
        products(count, d_right_ref, cube_ref, left_ref, True, False)
    d_left = d_left_ref[...]
    d_right = d_right_ref[...]
    d_proj = jnp.concatenate(
        [
            (d_left * sig_a).astype(jnp.bfloat16),
            (d_left * a_proj * sig_a * (1.0 - sig_a)).astype(jnp.bfloat16),
            (d_right * sig_b).astype(jnp.bfloat16),
            (d_right * b_proj * sig_b * (1.0 - sig_b)).astype(jnp.bfloat16),
        ],
        axis=1,
    )
    grads = (
        tn_dot(normed, d_proj) / count,
        tn_dot(normed, d_gate) / count,
        tn_dot(tri_norm, d_linear) / count,
    )
    return (d_proj, d_gate, grads, cot)


def pair_back(cot, pair, d_proj, d_gate, gain, w_proj, w_gate):
    pair_hat, pair_scale = normalize(pair, 1)
    d_normed = nt_dot(d_proj, w_proj) + nt_dot(d_gate, w_gate)
    return cot + norm_back(d_normed * gain, pair_hat, pair_scale, 1)


def second_kernel(shares, first_ref, second_ref, cot_ref, *rest):
    weight_refs, held, carried_ref, g_refs, weights = (
        rest[:5],
        rest[5],
        rest[6],
        rest[7:10],
        rest[10:15],
    )
    scratch, (stage_sem, weight_sem, send_sem, recv_sem) = rest[15:20], rest[20:]
    me = lax.axis_index("ax")
    count, channels = held.shape[3:]
    mesh_id = pl.DeviceIdType.MESH
    near_first = sorted(range(1, shares), key=lambda step: min(step, shares - step))
    barrier = pltpu.get_barrier_semaphore()
    for step in reversed(near_first):
        peer = lax.rem(me + step, shares)
        pl.semaphore_signal(barrier, inc=1, device_id={"ax": peer}, device_id_type=mesh_id)
    staged = []
    for place, ref in enumerate((second_ref, cot_ref, first_ref)):
        staged.append(pltpu.make_async_copy(ref, held.at[me, place], stage_sem.at[place]))
    loads = [
        pltpu.make_async_copy(ref, out, weight_sem.at[place])
        for place, (ref, out) in enumerate(zip(weight_refs, weights))
    ]
    for copy in staged + loads:
        copy.start()
    for copy in staged:
        copy.wait()
    pl.semaphore_wait(barrier, shares - 1)
    sends = []
    for place in range(3):
        group = []
        for step in reversed(near_first):
            peer = lax.rem(me + step, shares)
            copy = pltpu.make_async_remote_copy(
                src_ref=held.at[me, place],
                dst_ref=held.at[me, place],
                send_sem=send_sem.at[place, step],
                recv_sem=recv_sem.at[place, step],
                device_id={"ax": peer},
                device_id_type=mesh_id,
            )
            copy.start()
            group.append(copy)
        sends.append(group)
    for copy in loads:
        copy.wait()

    def arrived(place):
        for copy in sends[place]:
            copy.wait_recv()
        return held[:, place].reshape(-1, channels).astype(jnp.float32)

    second = arrived(0)
    d_proj, d_gate, grads, cot = crop_layer(
        1, True, count, second, lambda: arrived(1), *weights, *scratch
    )
    for ref, grad in zip(g_refs, grads):
        ref[...] = grad
    carried_ref[...] = pair_back(
        cot, second, d_proj, d_gate, weights[0][1:2, :], weights[1][1], weights[2][1]
    ).astype(jnp.bfloat16)
    for copy in sends[2]:
        copy.wait_recv()
    for group in sends:
        for copy in group:
            copy.wait_send()


def first_kernel(held, carried_ref, *rest):
    g_seconds, weights = rest[:3], rest[3:8]
    grad_in_ref, g_outs = rest[8], rest[9:12]
    g_firsts, scratch = rest[12:15], rest[15:20]
    d_proj_ref, d_gate_ref, first_sem, second_sem = rest[20:]
    rows, count, channels = held.shape[2:]
    copies = []
    for place in range(3):
        copies.append(
            pltpu.make_async_copy(g_seconds[place], g_outs[place].at[1], second_sem.at[place])
        )
        copies[-1].start()
    first = held[:, 2].reshape(-1, channels).astype(jnp.float32)
    d_proj, d_gate, grads, _ = crop_layer(
        0, False, count, first, lambda: carried_ref[...].astype(jnp.float32), *weights, *scratch
    )
    for place in range(3):
        g_firsts[place][...] = grads[place]
        copies.append(
            pltpu.make_async_copy(g_firsts[place], g_outs[place].at[0], first_sem.at[place])
        )
        copies[-1].start()
    d_proj_ref[...] = d_proj
    d_gate_ref[...] = d_gate
    me = lax.axis_index("ax")
    cells = rows * count
    mine = pl.ds(pl.multiple_of(me * cells, cells), cells)
    d_pair = pair_back(
        carried_ref[mine, :].astype(jnp.float32),
        held[me, 2].reshape(cells, channels).astype(jnp.float32),
        d_proj_ref[mine, :],
        d_gate_ref[mine, :],
        weights[0][0:1, :],
        weights[1][0],
        weights[2][0],
    )
    grad_in_ref[...] = d_pair.astype(jnp.bfloat16).reshape(grad_in_ref.shape)
    for copy in copies:
        copy.wait()


def whole_crop(
    pair_first, pair_second, grad_out, norm_gain, proj_weight, gate_weight, out_gain, out_weight
):
    shares = lax.axis_size("ax")
    rows, count, channels = pair_first.shape
    cells = count * count
    width = out_weight.shape[1]
    weights = (norm_gain, proj_weight, gate_weight, out_gain, out_weight)
    matrices = (proj_weight, gate_weight, out_weight)
    vmem = pl.BlockSpec(memory_space=pltpu.VMEM)
    hbm = pl.BlockSpec(memory_space=pltpu.HBM)
    f32 = jnp.float32
    cubes = [pltpu.VMEM((cells, width), f32) for _ in range(5)]
    args = (pair_first, pair_second, grad_out) + weights
    placed = pl.pallas_call(
        functools.partial(second_kernel, shares),
        out_shape=(
            pltpu.VMEM((shares, 3) + pair_first.shape, pair_first.dtype),
            pltpu.VMEM((cells, channels), jnp.bfloat16),
            *(pltpu.VMEM(matrix.shape[1:], f32) for matrix in matrices),
            *(pltpu.VMEM(weight.shape, weight.dtype) for weight in weights),
        ),
        in_specs=[hbm] * 8,
        out_specs=(vmem,) * 10,
        scratch_shapes=cubes
        + [
            pltpu.SemaphoreType.DMA((3,)),
            pltpu.SemaphoreType.DMA((5,)),
            pltpu.SemaphoreType.DMA((3, shares)),
            pltpu.SemaphoreType.DMA((3, shares)),
        ],
        compiler_params=pltpu.CompilerParams(
            collective_id=0, has_side_effects=True, vmem_limit_bytes=16 * 1024 * 1024
        ),
    )(*(pltpu.with_memory_space_constraint(arg, pltpu.HBM) for arg in args))
    return tuple(
        pl.pallas_call(
            first_kernel,
            out_shape=(
                jax.ShapeDtypeStruct(pair_first.shape, pair_first.dtype),
                *(jax.ShapeDtypeStruct(matrix.shape, f32) for matrix in matrices),
            ),
            in_specs=[vmem] * 10,
            out_specs=(vmem, hbm, hbm, hbm),
            scratch_shapes=[pltpu.VMEM(matrix.shape[1:], f32) for matrix in matrices]
            + cubes
            + [
                pltpu.VMEM((cells, 4 * width), jnp.bfloat16),
                pltpu.VMEM((cells, channels), jnp.bfloat16),
                pltpu.SemaphoreType.DMA((3,)),
                pltpu.SemaphoreType.DMA((3,)),
            ],
            compiler_params=pltpu.CompilerParams(vmem_limit_bytes=16 * 1024 * 1024),
        )(*placed)
    )


def on_device(*args):
    count = args[0].shape[1]
    if count % 16 == 0 and count <= 32:
        return whole_crop(*args)
    return split_crop(*args)


def solution(mesh):
    placed = (
        P(("grp", "ax"), None, None),
        P(("grp", "ax"), None, None),
        P(("grp", "ax"), None, None),
        P(),
        P(),
        P(),
        P(),
        P(),
    )
    return jax.shard_map(
        on_device,
        mesh=mesh,
        in_specs=placed,
        out_specs=(
            P(("grp", "ax"), None, None),
            P("grp", None, None),
            P("grp", None, None),
            P("grp", None, None),
        ),
        check_vma=False,
    )
```

```python
import functools

import jax
import jax.numpy as jnp
from jax import lax
from jax.experimental import pallas as pl
from jax.experimental.pallas import tpu as pltpu
from jax.sharding import PartitionSpec as P

EPS = 1e-05


def normalize(values, axis):
    center = values - jnp.mean(values, axis=axis, keepdims=True)
    scale = lax.rsqrt(jnp.mean(center * center, axis=axis, keepdims=True) + EPS)
    return (center * scale, scale)


def norm_back(grad, normed, scale, axis):
    return scale * (
        grad
        - jnp.mean(grad, axis=axis, keepdims=True)
        - normed * jnp.mean(grad * normed, axis=axis, keepdims=True)
    )


def own_cells(values):
    share = values.shape[1] // lax.axis_size("ch")
    return lax.dynamic_slice_in_dim(values, lax.axis_index("ch") * share, share, 1)


def front(pair, layer_gain, w_proj, w_gate):
    width = w_proj.shape[1] // 4
    rows = pair.shape[0]
    count = pair.shape[1]
    pair_hat, pair_scale = normalize(pair.astype(jnp.float32), 2)
    flat_normed = (pair_hat * layer_gain).astype(jnp.bfloat16).reshape(-1, pair.shape[2])
    projected = jnp.dot(flat_normed, w_proj, preferred_element_type=jnp.float32)
    gate_sig = jax.nn.sigmoid(jnp.dot(flat_normed, w_gate, preferred_element_type=jnp.float32))
    sig_a = jax.nn.sigmoid(projected[:, width : 2 * width])
    sig_b = jax.nn.sigmoid(projected[:, 3 * width :])
    left_side = (
        (sig_a * projected[:, :width])
        .astype(jnp.bfloat16)
        .reshape(rows, count, width)
        .transpose(2, 0, 1)
    )
    right_side = (
        (sig_b * projected[:, 2 * width : 3 * width])
        .astype(jnp.bfloat16)
        .reshape(rows, count, width)
        .transpose(2, 0, 1)
    )
    left_half, right_half = (
        lax.all_to_all(left_side, "ch", split_axis=0, concat_axis=2, tiled=True),
        lax.all_to_all(right_side, "ch", split_axis=0, concat_axis=2, tiled=True),
    )
    return (pair_hat, pair_scale, flat_normed, projected, gate_sig, left_half, right_half)


def rear(tri_half, gate_sig, cotangent, layer_out_gain, w_out):
    tri = lax.all_to_all(
        tri_half.astype(jnp.bfloat16), "ch", split_axis=2, concat_axis=0, tiled=True
    ).astype(tri_half.dtype)
    tri_hat, tri_scale = normalize(tri, 0)
    tri_norm = (tri_hat * layer_out_gain[:, None, None]).astype(jnp.bfloat16)
    linear = jnp.einsum("cij,cd->ijd", tri_norm, w_out, preferred_element_type=jnp.float32).reshape(
        -1, w_out.shape[1]
    )
    flat_cot = cotangent.reshape(-1, cotangent.shape[2])
    d_linear = (flat_cot * gate_sig).astype(jnp.bfloat16)
    d_gate = (flat_cot * linear * gate_sig * (1.0 - gate_sig)).astype(jnp.bfloat16)
    d_cube = d_linear.reshape(cotangent.shape[0], cotangent.shape[1], -1)
    d_norm = jnp.einsum("ijd,cd->cij", d_cube, w_out, preferred_element_type=jnp.float32)
    g_out = jnp.einsum("cij,ijd->cd", tri_norm, d_cube, preferred_element_type=jnp.float32)
    tri_grad = norm_back(d_norm * layer_out_gain[:, None, None], tri_hat, tri_scale, 0).astype(
        jnp.bfloat16
    )
    grad_half = lax.all_to_all(tri_grad, "ch", split_axis=0, concat_axis=2, tiled=True)
    return (grad_half, d_gate, g_out)


def front_back(
    cotangent,
    left_half_grad,
    right_half_grad,
    pair_hat,
    pair_scale,
    flat_normed,
    projected,
    d_gate,
    layer_gain,
    w_proj,
    w_gate,
):
    d_left, d_right = (
        lax.all_to_all(
            left_half_grad.astype(jnp.bfloat16), "ch", split_axis=2, concat_axis=0, tiled=True
        ).astype(left_half_grad.dtype),
        lax.all_to_all(
            right_half_grad.astype(jnp.bfloat16), "ch", split_axis=2, concat_axis=0, tiled=True
        ).astype(right_half_grad.dtype),
    )
    width = d_left.shape[0]
    sig_a = jax.nn.sigmoid(projected[:, width : 2 * width])
    sig_b = jax.nn.sigmoid(projected[:, 3 * width :])
    flat_left = d_left.transpose(1, 2, 0).reshape(-1, width)
    flat_right = d_right.transpose(1, 2, 0).reshape(-1, width)
    d_proj = jnp.concatenate(
        [
            flat_left * sig_a,
            flat_left * projected[:, :width] * sig_a * (1.0 - sig_a),
            flat_right * sig_b,
            flat_right * projected[:, 2 * width : 3 * width] * sig_b * (1.0 - sig_b),
        ],
        axis=1,
    ).astype(jnp.bfloat16)
    d_normed = jnp.dot(d_proj, w_proj.T, preferred_element_type=jnp.float32) + jnp.dot(
        d_gate, w_gate.T, preferred_element_type=jnp.float32
    )
    g_proj = jnp.einsum("nc,nd->cd", flat_normed, d_proj, preferred_element_type=jnp.float32)
    g_gate = jnp.einsum("nc,nd->cd", flat_normed, d_gate, preferred_element_type=jnp.float32)
    d_pair = cotangent + norm_back(
        d_normed.reshape(cotangent.shape) * layer_gain, pair_hat, pair_scale, 2
    )
    return (d_pair, g_proj, g_gate)


def outgoing(pair, cotangent, layer_gain, w_proj, w_gate, layer_out_gain, w_out):
    pair_hat, pair_scale, flat_normed, projected, gate_sig, left_half, right_half = front(
        pair, layer_gain, w_proj, w_gate
    )
    tri_half = jnp.einsum(
        "cik,cjk->cij",
        left_half,
        lax.all_gather(right_half, "ax", axis=1, tiled=True),
        preferred_element_type=jnp.float32,
    )
    grad_half, d_gate, g_out = rear(tri_half, gate_sig, cotangent, layer_out_gain, w_out)
    d_left = jnp.einsum(
        "cij,cjk->cik",
        grad_half,
        lax.all_gather(right_half, "ax", axis=1, tiled=True),
        preferred_element_type=jnp.float32,
    )
    turned = lax.all_to_all(grad_half, "ax", split_axis=2, concat_axis=1, tiled=True)
    d_right = jnp.einsum(
        "cij,cik->cjk",
        turned,
        lax.all_gather(left_half, "ax", axis=1, tiled=True),
        preferred_element_type=jnp.float32,
    )
    d_pair, g_proj, g_gate = front_back(
        cotangent,
        d_left,
        d_right,
        pair_hat,
        pair_scale,
        flat_normed,
        projected,
        d_gate,
        layer_gain,
        w_proj,
        w_gate,
    )
    return (d_pair, g_proj, g_gate, g_out)


def incoming(pair, cotangent, layer_gain, w_proj, w_gate, layer_out_gain, w_out):
    pair_hat, pair_scale, flat_normed, projected, gate_sig, left_half, right_half = front(
        pair, layer_gain, w_proj, w_gate
    )
    turned = lax.all_to_all(left_half, "ax", split_axis=2, concat_axis=1, tiled=True)
    part = turned
    tri_half = jnp.einsum(
        "cki,ckj->cij",
        part,
        lax.all_gather(right_half, "ax", axis=1, tiled=True),
        preferred_element_type=jnp.float32,
    )
    grad_half, d_gate, g_out = rear(tri_half, gate_sig, cotangent, layer_out_gain, w_out)
    d_turned = jnp.einsum(
        "ckj,cij->cki",
        lax.all_gather(right_half, "ax", axis=1, tiled=True),
        grad_half,
        preferred_element_type=jnp.float32,
    )
    d_left = lax.all_to_all(
        d_turned.astype(jnp.bfloat16), "ax", split_axis=1, concat_axis=2, tiled=True
    ).astype(d_turned.dtype)
    part = left_half
    d_right = jnp.einsum(
        "cki,cij->ckj",
        part,
        lax.all_gather(grad_half, "ax", axis=1, tiled=True),
        preferred_element_type=jnp.float32,
    )
    d_pair, g_proj, g_gate = front_back(
        cotangent,
        d_left,
        d_right,
        pair_hat,
        pair_scale,
        flat_normed,
        projected,
        d_gate,
        layer_gain,
        w_proj,
        w_gate,
    )
    return (d_pair, g_proj, g_gate, g_out)


def split_crop(
    pair_first, pair_second, grad_out, norm_gain, proj_weight, gate_weight, out_gain, out_weight
):
    count = pair_first.shape[1]
    second = incoming(
        own_cells(pair_second),
        own_cells(grad_out).astype(jnp.float32),
        norm_gain[1],
        proj_weight[1],
        gate_weight[1],
        out_gain[1],
        out_weight[1],
    )
    carried = lax.optimization_barrier(second[0].astype(jnp.bfloat16)).astype(jnp.float32)
    first = outgoing(
        own_cells(pair_first),
        carried,
        norm_gain[0],
        proj_weight[0],
        gate_weight[0],
        out_gain[0],
        out_weight[0],
    )
    totals = lax.psum(
        (
            jnp.stack([first[1], second[1]]),
            jnp.stack([first[2], second[2]]),
            jnp.stack([first[3], second[3]]),
        ),
        ("ax", "ch"),
    )
    grad_in = lax.all_gather(first[0].astype(jnp.bfloat16), "ch", axis=1, tiled=True)
    return (grad_in, totals[0] / count, totals[1] / count, totals[2] / count)


def nt_dot(a, b):
    return lax.dot_general(a, b, (((1,), (1,)), ((), ())), preferred_element_type=jnp.float32)


def tn_dot(a, b):
    return lax.dot_general(a, b, (((0,), (0,)), ((), ())), preferred_element_type=jnp.float32)


def gather_kernel(shares, halves, first_ref, second_ref, cot_ref, *rest):
    weight_refs, held, weight_outs = rest[:5], rest[5], rest[6:11]
    stage_sem, weight_sem, send_sem, recv_sem, pass_sem, got_sem = rest[11:]
    me = lax.axis_index("ax")
    core = lax.axis_index("ch")
    part = held.shape[3]
    mesh_id = pl.DeviceIdType.MESH
    near_first = sorted(range(1, shares), key=lambda step: min(step, shares - step))
    barrier = pltpu.get_barrier_semaphore()
    for step in reversed(near_first):
        peer = lax.rem(me + step, shares)
        pl.semaphore_signal(barrier, inc=1, device_id={"ax": peer}, device_id_type=mesh_id)
    for turn in range(1, halves):
        mate = lax.rem(core + turn, halves)
        pl.semaphore_signal(barrier, inc=1, device_id={"ch": mate}, device_id_type=mesh_id)
    staged = []
    for place, ref in enumerate((second_ref, cot_ref, first_ref)):
        for half in range(halves):
            copy = pltpu.make_async_copy(
                ref.at[pl.ds(half * part, part)],
                held.at[me, half, place],
                stage_sem.at[place, half],
            )
            copy.start()
            staged.append(copy)
    loads = [
        pltpu.make_async_copy(ref, out, weight_sem.at[place])
        for place, (ref, out) in enumerate(zip(weight_refs, weight_outs))
    ]
    for copy in staged:
        copy.wait()
    pl.semaphore_wait(barrier, shares + halves - 2)
    sends = {}
    for step in reversed(near_first):
        peer = lax.rem(me + step, shares)
        sends[step] = pltpu.make_async_remote_copy(
            src_ref=held.at[me, core],
            dst_ref=held.at[me, core],
            send_sem=send_sem.at[step],
            recv_sem=recv_sem.at[step],
            device_id={"ax": peer},
            device_id_type=mesh_id,
        )
        sends[step].start()
    for copy in loads:
        copy.start()
    passes = []
    for step in near_first:
        source = lax.rem(me - step + shares, shares)
        sends[step].wait_recv()
        for turn in range(1, halves):
            mate = lax.rem(core + turn, halves)
            copy = pltpu.make_async_remote_copy(
                src_ref=held.at[source, core],
                dst_ref=held.at[source, core],
                send_sem=pass_sem.at[step, turn],
                recv_sem=got_sem.at[step, turn],
                device_id={"ch": mate},
                device_id_type=mesh_id,
            )
            copy.start()
            passes.append(copy)
    for copy in passes:
        copy.wait_recv()
    for step in near_first:
        sends[step].wait_send()
    for copy in passes:
        copy.wait_send()
    for copy in loads:
        copy.wait()


def gather_rows(first, second, cot, weights, shares, halves):
    rows, count, channels = first.shape
    shape = (shares, halves, 3, rows // halves, count, channels)
    hbm = pl.BlockSpec(memory_space=pltpu.HBM)
    vmem = pl.BlockSpec(memory_space=pltpu.VMEM)
    return pl.pallas_call(
        functools.partial(gather_kernel, shares, halves),
        out_shape=(
            pltpu.VMEM(shape, first.dtype),
            *(pltpu.VMEM(weight.shape, weight.dtype) for weight in weights),
        ),
        in_specs=[hbm] * 8,
        out_specs=(vmem,) * 6,
        scratch_shapes=[
            pltpu.SemaphoreType.DMA((3, halves)),
            pltpu.SemaphoreType.DMA((5,)),
            pltpu.SemaphoreType.DMA((shares,)),
            pltpu.SemaphoreType.DMA((shares,)),
            pltpu.SemaphoreType.DMA((shares, halves)),
            pltpu.SemaphoreType.DMA((shares, halves)),
        ],
        compiler_params=pltpu.CompilerParams(
            collective_id=0, has_side_effects=True, vmem_limit_bytes=4 * 1024 * 1024
        ),
    )(*(pltpu.with_memory_space_constraint(x, pltpu.HBM) for x in (first, second, cot, *weights)))


def products(count, out_ref, a_ref, b_ref, a_swapped, b_swapped):
    block = 8
    for start in range(0, count, block):
        sums = [None] * block
        for r in range(count):
            if b_swapped:
                b = b_ref[pl.ds(r, count, stride=count), :]
            else:
                b = b_ref[r * count : (r + 1) * count, :]
            for place in range(block):
                p = start + place
                row = r * count + p if a_swapped else p * count + r
                term = a_ref[row : row + 1, :] * b
                sums[place] = term if sums[place] is None else sums[place] + term
        for place in range(block):
            p = start + place
            out_ref[p * count : (p + 1) * count, :] = sums[place]


def crop_layer(
    layer,
    incoming,
    count,
    pair,
    cot,
    gain_ref,
    proj_ref,
    gate_ref,
    out_gain_ref,
    out_w_ref,
    left_ref,
    right_ref,
    cube_ref,
    d_left_ref,
    d_right_ref,
):
    gain = gain_ref[layer : layer + 1, :]
    out_gain = out_gain_ref[layer : layer + 1, :]
    w_proj = proj_ref[layer]
    w_out = out_w_ref[layer]
    width = w_out.shape[0]
    pair_hat, pair_scale = normalize(pair, 1)
    normed = (pair_hat * gain).astype(jnp.bfloat16)
    projected = jnp.dot(normed, w_proj, preferred_element_type=jnp.float32)
    a_proj = projected[:, :width]
    b_proj = projected[:, 2 * width : 3 * width]
    sig_a = jax.nn.sigmoid(projected[:, width : 2 * width])
    sig_b = jax.nn.sigmoid(projected[:, 3 * width :])
    gate = jax.nn.sigmoid(jnp.dot(normed, gate_ref[layer], preferred_element_type=jnp.float32))
    left_ref[...] = (sig_a * a_proj).astype(jnp.bfloat16).astype(jnp.float32)
    right_ref[...] = (sig_b * b_proj).astype(jnp.bfloat16).astype(jnp.float32)
    if incoming:
        products(count, cube_ref, left_ref, right_ref, True, False)
    else:
        products(count, cube_ref, left_ref, right_ref, False, True)
    tri_hat, tri_scale = normalize(cube_ref[...], 1)
    tri_norm = (tri_hat * out_gain).astype(jnp.bfloat16)
    linear = jnp.dot(tri_norm, w_out, preferred_element_type=jnp.float32)
    scaled = cot * gate
    d_linear = scaled.astype(jnp.bfloat16)
    d_gate = (cot * linear * gate * (1.0 - gate)).astype(jnp.bfloat16)
    h = nt_dot(d_linear, w_out) * out_gain
    cube_ref[...] = (
        norm_back(h, tri_hat, tri_scale, 1).astype(jnp.bfloat16).astype(jnp.float32)
    )
    if incoming:
        products(count, d_left_ref, right_ref, cube_ref, False, True)
        products(count, d_right_ref, left_ref, cube_ref, False, False)
    else:
        products(count, d_left_ref, cube_ref, right_ref, False, False)
        products(count, d_right_ref, cube_ref, left_ref, True, False)
    d_left = d_left_ref[...]
    d_right = d_right_ref[...]
    d_proj = jnp.concatenate(
        [
            (d_left * sig_a).astype(jnp.bfloat16),
            (d_left * a_proj * sig_a * (1.0 - sig_a)).astype(jnp.bfloat16),
            (d_right * sig_b).astype(jnp.bfloat16),
            (d_right * b_proj * sig_b * (1.0 - sig_b)).astype(jnp.bfloat16),
        ],
        axis=1,
    )
    grads = (
        tn_dot(normed, d_proj) / count,
        tn_dot(normed, d_gate) / count,
        tn_dot(tri_norm, d_linear) / count,
    )
    return (d_proj, d_gate, grads)


def pair_back(cot, pair, d_proj, d_gate, gain, w_proj, w_gate):
    pair_hat, pair_scale = normalize(pair, 1)
    d_normed = nt_dot(d_proj, w_proj) + nt_dot(d_gate, w_gate)
    return cot + norm_back(d_normed * gain, pair_hat, pair_scale, 1)


def crop_kernel(
    held,
    gain_ref,
    proj_ref,
    gate_ref,
    out_gain_ref,
    out_w_ref,
    grad_in_ref,
    g_proj_ref,
    g_gate_ref,
    g_out_ref,
    left_ref,
    right_ref,
    cube_ref,
    d_left_ref,
    d_right_ref,
    carried_ref,
    d_proj_ref,
    d_gate_ref,
    held_g_proj,
    held_g_gate,
    held_g_out,
    write_sem,
):
    count, channels = held.shape[4:]
    rows = held.shape[1] * held.shape[3]
    scratch = (left_ref, right_ref, cube_ref, d_left_ref, d_right_ref)
    weights = (gain_ref, proj_ref, gate_ref, out_gain_ref, out_w_ref)
    second = held[:, :, 0].reshape(-1, channels).astype(jnp.float32)
    cot = held[:, :, 1].reshape(-1, channels).astype(jnp.float32)
    g_held = (held_g_proj, held_g_gate, held_g_out)
    g_outs = (g_proj_ref, g_gate_ref, g_out_ref)
    writes = []

    def write_out(layer, grads):
        for place in range(3):
            g_held[place][layer] = grads[place]
            writes.append(
                pltpu.make_async_copy(
                    g_held[place].at[layer], g_outs[place].at[layer], write_sem.at[layer, place]
                )
            )
            writes[-1].start()

    d_proj, d_gate, grads = crop_layer(1, True, count, second, cot, *weights, *scratch)
    write_out(1, grads)
    carried = pair_back(
        cot, second, d_proj, d_gate, gain_ref[1:2, :], proj_ref[1], gate_ref[1]
    ).astype(jnp.bfloat16)
    carried_ref[...] = carried
    first = held[:, :, 2].reshape(-1, channels).astype(jnp.float32)
    d_proj, d_gate, grads = crop_layer(
        0, False, count, first, carried.astype(jnp.float32), *weights, *scratch
    )
    write_out(0, grads)
    d_proj_ref[...] = d_proj
    d_gate_ref[...] = d_gate
    me = lax.axis_index("ax")
    cells = rows * count
    mine = pl.ds(pl.multiple_of(me * cells, cells), cells)
    d_pair = pair_back(
        carried_ref[mine, :].astype(jnp.float32),
        held[me, :, 2].reshape(cells, channels).astype(jnp.float32),
        d_proj_ref[mine, :],
        d_gate_ref[mine, :],
        gain_ref[0:1, :],
        proj_ref[0],
        gate_ref[0],
    )
    grad_in_ref[...] = d_pair.astype(jnp.bfloat16).reshape(grad_in_ref.shape)
    for copy in writes:
        copy.wait()


def whole_crop(
    pair_first, pair_second, grad_out, norm_gain, proj_weight, gate_weight, out_gain, out_weight
):
    shares = lax.axis_size("ax")
    rows, count, channels = pair_first.shape
    weights = (norm_gain, proj_weight, gate_weight, out_gain, out_weight)
    placed = gather_rows(
        pair_first, pair_second, grad_out, weights, shares, lax.axis_size("ch")
    )
    cells = count * count
    width = out_weight.shape[1]
    vmem = pl.BlockSpec(memory_space=pltpu.VMEM)
    hbm = pl.BlockSpec(memory_space=pltpu.HBM)
    f32 = jnp.float32
    return tuple(
        pl.pallas_call(
            crop_kernel,
            out_shape=(
                jax.ShapeDtypeStruct(pair_first.shape, pair_first.dtype),
                jax.ShapeDtypeStruct(proj_weight.shape, f32),
                jax.ShapeDtypeStruct(gate_weight.shape, f32),
                jax.ShapeDtypeStruct(out_weight.shape, f32),
            ),
            in_specs=[vmem] * 6,
            out_specs=(vmem,) + (hbm,) * 3,
            scratch_shapes=[
                pltpu.VMEM((cells, width), f32),
                pltpu.VMEM((cells, width), f32),
                pltpu.VMEM((cells, width), f32),
                pltpu.VMEM((cells, width), f32),
                pltpu.VMEM((cells, width), f32),
                pltpu.VMEM((cells, channels), jnp.bfloat16),
                pltpu.VMEM((cells, 4 * width), jnp.bfloat16),
                pltpu.VMEM((cells, channels), jnp.bfloat16),
                pltpu.VMEM(proj_weight.shape, f32),
                pltpu.VMEM(gate_weight.shape, f32),
                pltpu.VMEM(out_weight.shape, f32),
                pltpu.SemaphoreType.DMA((2, 3)),
            ],
            compiler_params=pltpu.CompilerParams(vmem_limit_bytes=16 * 1024 * 1024),
        )(*placed)
    )


def on_device(*args):
    rows, count = args[0].shape[:2]
    if count % 16 == 0 and count <= 32 and rows % lax.axis_size("ch") == 0:
        return whole_crop(*args)
    return split_crop(*args)


def solution(mesh):
    placed = (
        P(("grp", "ax"), None, None),
        P(("grp", "ax"), None, None),
        P(("grp", "ax"), None, None),
        P(),
        P(),
        P(),
        P(),
        P(),
    )
    return jax.shard_map(
        on_device,
        mesh=mesh,
        in_specs=placed,
        out_specs=(
            P(("grp", "ax"), None, None),
            P("grp", None, None),
            P("grp", None, None),
            P("grp", None, None),
        ),
        check_vma=False,
    )
```

```python
import functools

import jax
import jax.numpy as jnp
from jax import lax
from jax.experimental import pallas as pl
from jax.experimental.pallas import tpu as pltpu
from jax.sharding import PartitionSpec as P

EPS = 1e-05


def normalize(values, axis):
    center = values - jnp.mean(values, axis=axis, keepdims=True)
    scale = lax.rsqrt(jnp.mean(center * center, axis=axis, keepdims=True) + EPS)
    return (center * scale, scale)


def norm_back(grad, normed, scale, axis):
    return scale * (
        grad
        - jnp.mean(grad, axis=axis, keepdims=True)
        - normed * jnp.mean(grad * normed, axis=axis, keepdims=True)
    )


def own_cells(values):
    share = values.shape[1] // lax.axis_size("ch")
    return lax.dynamic_slice_in_dim(values, lax.axis_index("ch") * share, share, 1)


def front(pair, layer_gain, w_proj, w_gate):
    width = w_proj.shape[1] // 4
    rows = pair.shape[0]
    count = pair.shape[1]
    pair_hat, pair_scale = normalize(pair.astype(jnp.float32), 2)
    flat_normed = (pair_hat * layer_gain).astype(jnp.bfloat16).reshape(-1, pair.shape[2])
    projected = jnp.dot(flat_normed, w_proj, preferred_element_type=jnp.float32)
    gate_sig = jax.nn.sigmoid(jnp.dot(flat_normed, w_gate, preferred_element_type=jnp.float32))
    sig_a = jax.nn.sigmoid(projected[:, width : 2 * width])
    sig_b = jax.nn.sigmoid(projected[:, 3 * width :])
    left_side = (
        (sig_a * projected[:, :width])
        .astype(jnp.bfloat16)
        .reshape(rows, count, width)
        .transpose(2, 0, 1)
    )
    right_side = (
        (sig_b * projected[:, 2 * width : 3 * width])
        .astype(jnp.bfloat16)
        .reshape(rows, count, width)
        .transpose(2, 0, 1)
    )
    left_half, right_half = (
        lax.all_to_all(left_side, "ch", split_axis=0, concat_axis=2, tiled=True),
        lax.all_to_all(right_side, "ch", split_axis=0, concat_axis=2, tiled=True),
    )
    return (pair_hat, pair_scale, flat_normed, projected, gate_sig, left_half, right_half)


def rear(tri_half, gate_sig, cotangent, layer_out_gain, w_out):
    tri = lax.all_to_all(
        tri_half.astype(jnp.bfloat16), "ch", split_axis=2, concat_axis=0, tiled=True
    ).astype(tri_half.dtype)
    tri_hat, tri_scale = normalize(tri, 0)
    tri_norm = (tri_hat * layer_out_gain[:, None, None]).astype(jnp.bfloat16)
    linear = jnp.einsum("cij,cd->ijd", tri_norm, w_out, preferred_element_type=jnp.float32).reshape(
        -1, w_out.shape[1]
    )
    flat_cot = cotangent.reshape(-1, cotangent.shape[2])
    d_linear = (flat_cot * gate_sig).astype(jnp.bfloat16)
    d_gate = (flat_cot * linear * gate_sig * (1.0 - gate_sig)).astype(jnp.bfloat16)
    d_cube = d_linear.reshape(cotangent.shape[0], cotangent.shape[1], -1)
    d_norm = jnp.einsum("ijd,cd->cij", d_cube, w_out, preferred_element_type=jnp.float32)
    g_out = jnp.einsum("cij,ijd->cd", tri_norm, d_cube, preferred_element_type=jnp.float32)
    tri_grad = norm_back(d_norm * layer_out_gain[:, None, None], tri_hat, tri_scale, 0).astype(
        jnp.bfloat16
    )
    grad_half = lax.all_to_all(tri_grad, "ch", split_axis=0, concat_axis=2, tiled=True)
    return (grad_half, d_gate, g_out)


def front_back(
    cotangent,
    left_half_grad,
    right_half_grad,
    pair_hat,
    pair_scale,
    flat_normed,
    projected,
    d_gate,
    layer_gain,
    w_proj,
    w_gate,
):
    d_left, d_right = (
        lax.all_to_all(
            left_half_grad.astype(jnp.bfloat16), "ch", split_axis=2, concat_axis=0, tiled=True
        ).astype(left_half_grad.dtype),
        lax.all_to_all(
            right_half_grad.astype(jnp.bfloat16), "ch", split_axis=2, concat_axis=0, tiled=True
        ).astype(right_half_grad.dtype),
    )
    width = d_left.shape[0]
    sig_a = jax.nn.sigmoid(projected[:, width : 2 * width])
    sig_b = jax.nn.sigmoid(projected[:, 3 * width :])
    flat_left = d_left.transpose(1, 2, 0).reshape(-1, width)
    flat_right = d_right.transpose(1, 2, 0).reshape(-1, width)
    d_proj = jnp.concatenate(
        [
            flat_left * sig_a,
            flat_left * projected[:, :width] * sig_a * (1.0 - sig_a),
            flat_right * sig_b,
            flat_right * projected[:, 2 * width : 3 * width] * sig_b * (1.0 - sig_b),
        ],
        axis=1,
    ).astype(jnp.bfloat16)
    d_normed = jnp.dot(d_proj, w_proj.T, preferred_element_type=jnp.float32) + jnp.dot(
        d_gate, w_gate.T, preferred_element_type=jnp.float32
    )
    g_proj = jnp.einsum("nc,nd->cd", flat_normed, d_proj, preferred_element_type=jnp.float32)
    g_gate = jnp.einsum("nc,nd->cd", flat_normed, d_gate, preferred_element_type=jnp.float32)
    d_pair = cotangent + norm_back(
        d_normed.reshape(cotangent.shape) * layer_gain, pair_hat, pair_scale, 2
    )
    return (d_pair, g_proj, g_gate)


def outgoing(pair, cotangent, layer_gain, w_proj, w_gate, layer_out_gain, w_out):
    pair_hat, pair_scale, flat_normed, projected, gate_sig, left_half, right_half = front(
        pair, layer_gain, w_proj, w_gate
    )
    tri_half = jnp.einsum(
        "cik,cjk->cij",
        left_half,
        lax.all_gather(right_half, "ax", axis=1, tiled=True),
        preferred_element_type=jnp.float32,
    )
    grad_half, d_gate, g_out = rear(tri_half, gate_sig, cotangent, layer_out_gain, w_out)
    d_left = jnp.einsum(
        "cij,cjk->cik",
        grad_half,
        lax.all_gather(right_half, "ax", axis=1, tiled=True),
        preferred_element_type=jnp.float32,
    )
    turned = lax.all_to_all(grad_half, "ax", split_axis=2, concat_axis=1, tiled=True)
    d_right = jnp.einsum(
        "cij,cik->cjk",
        turned,
        lax.all_gather(left_half, "ax", axis=1, tiled=True),
        preferred_element_type=jnp.float32,
    )
    d_pair, g_proj, g_gate = front_back(
        cotangent,
        d_left,
        d_right,
        pair_hat,
        pair_scale,
        flat_normed,
        projected,
        d_gate,
        layer_gain,
        w_proj,
        w_gate,
    )
    return (d_pair, g_proj, g_gate, g_out)


def incoming(pair, cotangent, layer_gain, w_proj, w_gate, layer_out_gain, w_out):
    pair_hat, pair_scale, flat_normed, projected, gate_sig, left_half, right_half = front(
        pair, layer_gain, w_proj, w_gate
    )
    turned = lax.all_to_all(left_half, "ax", split_axis=2, concat_axis=1, tiled=True)
    part = turned
    tri_half = jnp.einsum(
        "cki,ckj->cij",
        part,
        lax.all_gather(right_half, "ax", axis=1, tiled=True),
        preferred_element_type=jnp.float32,
    )
    grad_half, d_gate, g_out = rear(tri_half, gate_sig, cotangent, layer_out_gain, w_out)
    d_turned = jnp.einsum(
        "ckj,cij->cki",
        lax.all_gather(right_half, "ax", axis=1, tiled=True),
        grad_half,
        preferred_element_type=jnp.float32,
    )
    d_left = lax.all_to_all(
        d_turned.astype(jnp.bfloat16), "ax", split_axis=1, concat_axis=2, tiled=True
    ).astype(d_turned.dtype)
    part = left_half
    d_right = jnp.einsum(
        "cki,cij->ckj",
        part,
        lax.all_gather(grad_half, "ax", axis=1, tiled=True),
        preferred_element_type=jnp.float32,
    )
    d_pair, g_proj, g_gate = front_back(
        cotangent,
        d_left,
        d_right,
        pair_hat,
        pair_scale,
        flat_normed,
        projected,
        d_gate,
        layer_gain,
        w_proj,
        w_gate,
    )
    return (d_pair, g_proj, g_gate, g_out)


def split_crop(
    pair_first, pair_second, grad_out, norm_gain, proj_weight, gate_weight, out_gain, out_weight
):
    count = pair_first.shape[1]
    second = incoming(
        own_cells(pair_second),
        own_cells(grad_out).astype(jnp.float32),
        norm_gain[1],
        proj_weight[1],
        gate_weight[1],
        out_gain[1],
        out_weight[1],
    )
    carried = lax.optimization_barrier(second[0].astype(jnp.bfloat16)).astype(jnp.float32)
    first = outgoing(
        own_cells(pair_first),
        carried,
        norm_gain[0],
        proj_weight[0],
        gate_weight[0],
        out_gain[0],
        out_weight[0],
    )
    totals = lax.psum(
        (
            jnp.stack([first[1], second[1]]),
            jnp.stack([first[2], second[2]]),
            jnp.stack([first[3], second[3]]),
        ),
        ("ax", "ch"),
    )
    grad_in = lax.all_gather(first[0].astype(jnp.bfloat16), "ch", axis=1, tiled=True)
    return (grad_in, totals[0] / count, totals[1] / count, totals[2] / count)


def nt_dot(a, b):
    return lax.dot_general(a, b, (((1,), (1,)), ((), ())), preferred_element_type=jnp.float32)


def tn_dot(a, b):
    return lax.dot_general(a, b, (((0,), (0,)), ((), ())), preferred_element_type=jnp.float32)


def gather_kernel(shares, halves, first_ref, second_ref, cot_ref, *rest):
    weight_refs, held, weight_outs = rest[:5], rest[5], rest[6:11]
    stage_sem, weight_sem, send_sem, recv_sem, pass_sem, got_sem = rest[11:]
    me = lax.axis_index("ax")
    core = lax.axis_index("ch")
    part = held.shape[3]
    mesh_id = pl.DeviceIdType.MESH
    near_first = sorted(range(1, shares), key=lambda step: min(step, shares - step))
    barrier = pltpu.get_barrier_semaphore()
    for step in reversed(near_first):
        peer = lax.rem(me + step, shares)
        pl.semaphore_signal(barrier, inc=1, device_id={"ax": peer}, device_id_type=mesh_id)
    for turn in range(1, halves):
        mate = lax.rem(core + turn, halves)
        pl.semaphore_signal(barrier, inc=1, device_id={"ch": mate}, device_id_type=mesh_id)
    staged = []
    for place, ref in enumerate((second_ref, cot_ref, first_ref)):
        for half in range(halves):
            copy = pltpu.make_async_copy(
                ref.at[pl.ds(half * part, part)],
                held.at[me, half, place],
                stage_sem.at[place, half],
            )
            copy.start()
            staged.append(copy)
    loads = [
        pltpu.make_async_copy(ref, out, weight_sem.at[place])
        for place, (ref, out) in enumerate(zip(weight_refs, weight_outs))
    ]
    for copy in loads:
        copy.start()
    for copy in staged:
        copy.wait()
    pl.semaphore_wait(barrier, shares + halves - 2)
    sends = {}
    for step in reversed(near_first):
        peer = lax.rem(me + step, shares)
        sends[step] = pltpu.make_async_remote_copy(
            src_ref=held.at[me, core],
            dst_ref=held.at[me, core],
            send_sem=send_sem.at[step],
            recv_sem=recv_sem.at[step],
            device_id={"ax": peer},
            device_id_type=mesh_id,
        )
        sends[step].start()
    passes = []
    for step in near_first:
        source = lax.rem(me - step + shares, shares)
        sends[step].wait_recv()
        for turn in range(1, halves):
            mate = lax.rem(core + turn, halves)
            copy = pltpu.make_async_remote_copy(
                src_ref=held.at[source, core],
                dst_ref=held.at[source, core],
                send_sem=pass_sem.at[step, turn],
                recv_sem=got_sem.at[step, turn],
                device_id={"ch": mate},
                device_id_type=mesh_id,
            )
            copy.start()
            passes.append(copy)
    for copy in passes:
        copy.wait_recv()
    for step in near_first:
        sends[step].wait_send()
    for copy in passes:
        copy.wait_send()
    for copy in loads:
        copy.wait()


def gather_rows(first, second, cot, weights, shares, halves):
    rows, count, channels = first.shape
    shape = (shares, halves, 3, rows // halves, count, channels)
    hbm = pl.BlockSpec(memory_space=pltpu.HBM)
    vmem = pl.BlockSpec(memory_space=pltpu.VMEM)
    return pl.pallas_call(
        functools.partial(gather_kernel, shares, halves),
        out_shape=(
            pltpu.VMEM(shape, first.dtype),
            *(pltpu.VMEM(weight.shape, weight.dtype) for weight in weights),
        ),
        in_specs=[hbm] * 8,
        out_specs=(vmem,) * 6,
        scratch_shapes=[
            pltpu.SemaphoreType.DMA((3, halves)),
            pltpu.SemaphoreType.DMA((5,)),
            pltpu.SemaphoreType.DMA((shares,)),
            pltpu.SemaphoreType.DMA((shares,)),
            pltpu.SemaphoreType.DMA((shares, halves)),
            pltpu.SemaphoreType.DMA((shares, halves)),
        ],
        compiler_params=pltpu.CompilerParams(
            collective_id=0, has_side_effects=True, vmem_limit_bytes=4 * 1024 * 1024
        ),
    )(*(pltpu.with_memory_space_constraint(x, pltpu.HBM) for x in (first, second, cot, *weights)))


def products(count, out_ref, a_ref, b_ref, a_swapped, b_swapped):
    block = 16
    for start in range(0, count, block):
        sums = [None] * block
        for r in range(count):
            if b_swapped:
                b = b_ref[pl.ds(r, count, stride=count), :]
            else:
                b = b_ref[r * count : (r + 1) * count, :]
            for place in range(block):
                p = start + place
                row = r * count + p if a_swapped else p * count + r
                term = a_ref[row : row + 1, :] * b
                sums[place] = term if sums[place] is None else sums[place] + term
        for place in range(block):
            p = start + place
            out_ref[p * count : (p + 1) * count, :] = sums[place]


def crop_layer(
    layer,
    incoming,
    count,
    pair,
    cot,
    gain_ref,
    proj_ref,
    gate_ref,
    out_gain_ref,
    out_w_ref,
    left_ref,
    right_ref,
    cube_ref,
    d_left_ref,
    d_right_ref,
):
    gain = gain_ref[layer : layer + 1, :]
    out_gain = out_gain_ref[layer : layer + 1, :]
    w_proj = proj_ref[layer]
    w_out = out_w_ref[layer]
    width = w_out.shape[0]
    pair_hat, pair_scale = normalize(pair, 1)
    normed = (pair_hat * gain).astype(jnp.bfloat16)
    projected = jnp.dot(normed, w_proj, preferred_element_type=jnp.float32)
    a_proj = projected[:, :width]
    b_proj = projected[:, 2 * width : 3 * width]
    sig_a = jax.nn.sigmoid(projected[:, width : 2 * width])
    sig_b = jax.nn.sigmoid(projected[:, 3 * width :])
    gate = jax.nn.sigmoid(jnp.dot(normed, gate_ref[layer], preferred_element_type=jnp.float32))
    left_ref[...] = (sig_a * a_proj).astype(jnp.bfloat16).astype(jnp.float32)
    right_ref[...] = (sig_b * b_proj).astype(jnp.bfloat16).astype(jnp.float32)
    if incoming:
        products(count, cube_ref, left_ref, right_ref, True, False)
    else:
        products(count, cube_ref, left_ref, right_ref, False, True)
    tri_hat, tri_scale = normalize(cube_ref[...], 1)
    tri_norm = (tri_hat * out_gain).astype(jnp.bfloat16)
    linear = jnp.dot(tri_norm, w_out, preferred_element_type=jnp.float32)
    scaled = cot * gate
    d_linear = scaled.astype(jnp.bfloat16)
    d_gate = (cot * linear * gate * (1.0 - gate)).astype(jnp.bfloat16)
    h = nt_dot(d_linear, w_out) * out_gain
    cube_ref[...] = (
        norm_back(h, tri_hat, tri_scale, 1).astype(jnp.bfloat16).astype(jnp.float32)
    )
    if incoming:
        products(count, d_left_ref, right_ref, cube_ref, False, True)
        products(count, d_right_ref, left_ref, cube_ref, False, False)
    else:
        products(count, d_left_ref, cube_ref, right_ref, False, False)
        products(count, d_right_ref, cube_ref, left_ref, True, False)
    d_left = d_left_ref[...]
    d_right = d_right_ref[...]
    d_proj = jnp.concatenate(
        [
            (d_left * sig_a).astype(jnp.bfloat16),
            (d_left * a_proj * sig_a * (1.0 - sig_a)).astype(jnp.bfloat16),
            (d_right * sig_b).astype(jnp.bfloat16),
            (d_right * b_proj * sig_b * (1.0 - sig_b)).astype(jnp.bfloat16),
        ],
        axis=1,
    )
    grads = (
        tn_dot(normed, d_proj) / count,
        tn_dot(normed, d_gate) / count,
        tn_dot(tri_norm, d_linear) / count,
    )
    return (d_proj, d_gate, grads)


def pair_back(cot, pair, d_proj, d_gate, gain, w_proj, w_gate):
    pair_hat, pair_scale = normalize(pair, 1)
    d_normed = nt_dot(d_proj, w_proj) + nt_dot(d_gate, w_gate)
    return cot + norm_back(d_normed * gain, pair_hat, pair_scale, 1)


def crop_kernel(
    held,
    gain_ref,
    proj_ref,
    gate_ref,
    out_gain_ref,
    out_w_ref,
    grad_in_ref,
    g_proj_ref,
    g_gate_ref,
    g_out_ref,
    left_ref,
    right_ref,
    cube_ref,
    d_left_ref,
    d_right_ref,
    carried_ref,
    d_proj_ref,
    d_gate_ref,
):
    count, channels = held.shape[4:]
    rows = held.shape[1] * held.shape[3]
    scratch = (left_ref, right_ref, cube_ref, d_left_ref, d_right_ref)
    weights = (gain_ref, proj_ref, gate_ref, out_gain_ref, out_w_ref)
    second = held[:, :, 0].reshape(-1, channels).astype(jnp.float32)
    cot = held[:, :, 1].reshape(-1, channels).astype(jnp.float32)
    d_proj, d_gate, grads = crop_layer(1, True, count, second, cot, *weights, *scratch)
    g_proj_ref[1], g_gate_ref[1], g_out_ref[1] = grads
    carried = pair_back(
        cot, second, d_proj, d_gate, gain_ref[1:2, :], proj_ref[1], gate_ref[1]
    ).astype(jnp.bfloat16)
    carried_ref[...] = carried
    first = held[:, :, 2].reshape(-1, channels).astype(jnp.float32)
    d_proj, d_gate, grads = crop_layer(
        0, False, count, first, carried.astype(jnp.float32), *weights, *scratch
    )
    g_proj_ref[0], g_gate_ref[0], g_out_ref[0] = grads
    d_proj_ref[...] = d_proj
    d_gate_ref[...] = d_gate
    me = lax.axis_index("ax")
    cells = rows * count
    mine = pl.ds(pl.multiple_of(me * cells, cells), cells)
    d_pair = pair_back(
        carried_ref[mine, :].astype(jnp.float32),
        held[me, :, 2].reshape(cells, channels).astype(jnp.float32),
        d_proj_ref[mine, :],
        d_gate_ref[mine, :],
        gain_ref[0:1, :],
        proj_ref[0],
        gate_ref[0],
    )
    grad_in_ref[...] = d_pair.astype(jnp.bfloat16).reshape(grad_in_ref.shape)


def whole_crop(
    pair_first, pair_second, grad_out, norm_gain, proj_weight, gate_weight, out_gain, out_weight
):
    shares = lax.axis_size("ax")
    rows, count, channels = pair_first.shape
    weights = (norm_gain, proj_weight, gate_weight, out_gain, out_weight)
    placed = gather_rows(
        pair_first, pair_second, grad_out, weights, shares, lax.axis_size("ch")
    )
    cells = count * count
    width = out_weight.shape[1]
    vmem = pl.BlockSpec(memory_space=pltpu.VMEM)
    f32 = jnp.float32
    return tuple(
        pl.pallas_call(
            crop_kernel,
            out_shape=(
                jax.ShapeDtypeStruct(pair_first.shape, pair_first.dtype),
                jax.ShapeDtypeStruct(proj_weight.shape, f32),
                jax.ShapeDtypeStruct(gate_weight.shape, f32),
                jax.ShapeDtypeStruct(out_weight.shape, f32),
            ),
            in_specs=[vmem] * 6,
            out_specs=(vmem,) * 4,
            scratch_shapes=[
                pltpu.VMEM((cells, width), f32),
                pltpu.VMEM((cells, width), f32),
                pltpu.VMEM((cells, width), f32),
                pltpu.VMEM((cells, width), f32),
                pltpu.VMEM((cells, width), f32),
                pltpu.VMEM((cells, channels), jnp.bfloat16),
                pltpu.VMEM((cells, 4 * width), jnp.bfloat16),
                pltpu.VMEM((cells, channels), jnp.bfloat16),
            ],
            compiler_params=pltpu.CompilerParams(vmem_limit_bytes=16 * 1024 * 1024),
        )(*placed)
    )


def on_device(*args):
    rows, count = args[0].shape[:2]
    if count % 16 == 0 and count <= 32 and rows % lax.axis_size("ch") == 0:
        return whole_crop(*args)
    return split_crop(*args)


def solution(mesh):
    placed = (
        P(("grp", "ax"), None, None),
        P(("grp", "ax"), None, None),
        P(("grp", "ax"), None, None),
        P(),
        P(),
        P(),
        P(),
        P(),
    )
    return jax.shard_map(
        on_device,
        mesh=mesh,
        in_specs=placed,
        out_specs=(
            P(("grp", "ax"), None, None),
            P("grp", None, None),
            P("grp", None, None),
            P("grp", None, None),
        ),
        check_vma=False,
    )
```
